32 devices in a mesh: dp: 16 (over z, y, x), frame: 2 (over core).
Axes of the slice: x: 2, y: 2, z: 4, core: 2. Of those that a mesh axis runs over, the one named last changes fastest.
Arguments:
- tokens: bfloat16 [2, 16, 2, 256, 1024], P(None, 'dp', 'frame'), may hold values from -6 to 6
- memory: bfloat16 [2, 16, 2, 256, 1024], P(None, 'dp', None, 'frame'), may hold values from -6 to 6
- token_lengths: int32 [2, 16, 2, 4], P(None, 'dp'), may hold values from 1 to 128, 256 in all within a row
- frame_lengths: int32 [2, 16, 2, 4], P(None, 'dp'), may hold values from 1 to 192, 256 in all within a row
- attention_in: bfloat16 [2, 3, 1024, 1024], replicated, may hold values from -0.1875 to 0.1875
- attention_out: bfloat16 [2, 1024, 1024], replicated, may hold values from -0.75 to 0.75
- attention_bias: float32 [2, 3, 1024], replicated, may hold values from -1.5 to 1.5
- norm_gain: float32 [4, 1024], replicated, may hold values from 0.25 to 1.75
- norm_bias: float32 [4, 1024], replicated, may hold values from -1.5 to 1.5
- expand_weight: bfloat16 [1024, 4096], replicated, may hold values from -0.1875 to 0.1875
- expand_bias: float32 [4096], replicated, may hold values from -1.5 to 1.5
- reduce_weight: bfloat16 [4096, 1024], replicated, may hold values from -0.1875 to 0.1875
- reduce_bias: float32 [1024], replicated, may hold values from -1.5 to 1.5
- cotangent: bfloat16 [2, 16, 2, 256, 1024], P(None, 'dp', 'frame'), may hold values from -6 to 6
Outputs:
- out_tokens: bfloat16 [2, 16, 2, 256, 1024], P(None, 'dp', 'frame')
- grad_tokens: float32 [2, 16, 2, 256, 1024], P(None, 'dp', 'frame')
- grad_memory: float32 [2, 16, 2, 256, 1024], P(None, 'dp', None, 'frame')
- grad_attention_in: float32 [2, 3, 1024, 1024], P(None, None, ('dp', 'frame'))
- grad_attention_out: float32 [2, 1024, 1024], P(None, ('dp', 'frame'))
- grad_attention_bias: float32 [2, 3, 1024], P(None, None, ('dp', 'frame'))
- grad_norm_gain: float32 [4, 1024], P(None, ('dp', 'frame'))
- grad_norm_bias: float32 [4, 1024], P(None, ('dp', 'frame'))
- grad_expand_weight: float32 [1024, 4096], P(('dp', 'frame'))
- grad_expand_bias: float32 [4096], P(('dp', 'frame'))
- grad_reduce_weight: float32 [4096, 1024], P(('dp', 'frame'))
- grad_reduce_bias: float32 [1024], P(('dp', 'frame'))
The draws below stay inside these ranges and needn't reach their ends.
Inputs may be any that keep to these rules, and one draw needn't show every extreme that they name: `token_lengths`: each list of 4 lengths sums to 256, and its longest is 128. `frame_lengths`: each list of 4 lengths sums to 256, and its longest is 192.
All inputs are finite; a program needn't handle non-finite values.
Results may differ from the reference program's by a relative error of at most 0.015.
Values may be sent and summed in bfloat16 or wider, within the bound.
A program may use at most 320 MiB of HBM per device.

```python
import math
import jax
import jax.numpy as jnp
import numpy as np
from jax import lax

D = 1024
FF = 4096
HEADS = 16
HEAD_DIM = 64
ROWS = 256
MEM = 256
NSEQ = 4
MB = 2
PAIRS = 16
HALVES = 2
TOK_MOST = 128
MEM_MOST = 192


def steps_of(rng, dims, split, low, largest):
    loudness = 1.0
    for dim, shards_of in split:
        steps = jax.random.uniform(jax.random.fold_in(jax.random.fold_in(rng, 6), dim), (shards_of,), jnp.float32, low / len(split), largest / len(split))
        loudness = loudness * jnp.repeat(jnp.exp(steps), dims[dim] // shards_of).reshape((-1,) + (1,) * (len(dims) - 1 - dim))
    return loudness


def split_up(number_of, total, limit, skew):
    loads = [(1 << 20) // math.isqrt(standing ** skew) + 1 for standing in range(2, number_of + 1)]
    spare, given = total - limit - (number_of - 1), [1] * (number_of - 1)
    while spare > 0:
        candidates = [i for i in range(number_of - 1) if given[i] < limit]
        mass, left = sum([loads[i] for i in candidates]), spare
        for i in candidates:
            extra = min(limit - given[i], max(1, left * loads[i] // mass), spare)
            given[i] = given[i] + extra
            spare = spare - extra
    return np.array([limit] + given)


def uneven_parts(stream_key, number_of, total, limit, lean):
    if number_of == 2:
        one = jax.random.randint(stream_key, (), max(1, total - limit), min(limit, total - 1) + 1)
        return jnp.stack([one, total - one])
    tallies = jnp.asarray(split_up(number_of, total, limit, lean), jnp.int32)
    couples = (number_of - 1) // 2
    donor, taker = tallies[1:1 + 2 * couples:2], tallies[2:2 + 2 * couples:2]
    margin = jnp.minimum(donor - 1, limit - taker)
    shifted = jax.random.randint(jax.random.fold_in(stream_key, 1), (couples,), 0, 1 << 20) % (margin + 1)
    tallies = tallies.at[1:1 + 2 * couples:2].set(donor - shifted).at[2:2 + 2 * couples:2].set(taker + shifted)
    return tallies[jax.random.permutation(jax.random.fold_in(stream_key, 2), number_of)]


def bell_draw(stream_key, extent, width, limit, split=(), kind=jnp.bfloat16):
    array = jax.random.normal(stream_key, extent, jnp.float32) * width
    if len(split) > 0:
        array = steps_of(stream_key, extent, split, -0.22, 0.18) * array
    return jnp.clip(array, min=-limit, max=limit).astype(kind)


def setup_inputs(seed: int = 0) -> dict:
    key_list = jax.random.split(jax.random.key(seed), 15)
    tokens = bell_draw(key_list[0], (MB, PAIRS, HALVES, ROWS, D), 1.0, 6.0, ((1, 16), (2, 2)))
    memory = bell_draw(key_list[1], (MB, PAIRS, HALVES, MEM, D), 1.0, 6.0, ((1, 16), (3, 2)))
    token_lengths = jax.vmap(lambda own: uneven_parts(own, NSEQ, ROWS, TOK_MOST, 2))(jax.random.split(key_list[2], MB * PAIRS * HALVES)).reshape((MB, PAIRS, HALVES, NSEQ)).astype(jnp.int32)
    frame_lengths = jax.vmap(lambda own: uneven_parts(own, NSEQ, MEM, MEM_MOST, 2))(jax.random.split(key_list[3], MB * PAIRS * HALVES)).reshape((MB, PAIRS, HALVES, NSEQ)).astype(jnp.int32)
    attention_in = bell_draw(key_list[4], (2, 3, D, D), D ** -0.5, 0.1875)
    attention_out = bell_draw(key_list[5], (2, D, D), (D // 16) ** -0.5, 0.75)
    attention_bias = bell_draw(key_list[6], (2, 3, D), 0.3, 1.5, (), jnp.float32)
    norm_gain = jnp.clip(1.0 + 0.15 * jax.random.normal(key_list[7], (4, D), jnp.float32), 0.25, 1.75)
    norm_bias = bell_draw(key_list[8], (4, D), 0.3, 1.5, (), jnp.float32)
    expand_weight = bell_draw(key_list[9], (D, FF), D ** -0.5, 0.1875)
    expand_bias = bell_draw(key_list[10], (FF,), 0.3, 1.5, (), jnp.float32)
    reduce_weight = bell_draw(key_list[11], (FF, D), (FF // 4) ** -0.5, 0.1875)
    reduce_bias = bell_draw(key_list[12], (D,), 0.3, 1.5, (), jnp.float32)
    cotangent = bell_draw(key_list[13], (MB, PAIRS, HALVES, ROWS, D), 1.0, 6.0, ((1, 16), (2, 2)))
    return dict(tokens=tokens, memory=memory, token_lengths=token_lengths, frame_lengths=frame_lengths, attention_in=attention_in, attention_out=attention_out, attention_bias=attention_bias, norm_gain=norm_gain, norm_bias=norm_bias, expand_weight=expand_weight, expand_bias=expand_bias, reduce_weight=reduce_weight, reduce_bias=reduce_bias, cotangent=cotangent)


@jax.custom_vjp
def low(v):
    return lax.optimization_barrier(v.astype(jnp.bfloat16)).astype(jnp.float32)

@jax.custom_vjp
def low_back(v):
    return v

def low_keep(v):
    return (low(v), None)

def low_pass(kept, grad):
    return (grad,)

def back_keep(v):
    return (v, None)

def back_low(kept, grad):
    return (low(grad),)
low.defvjp(low_keep, low_pass)
low_back.defvjp(back_keep, back_low)

def both_ways(value):
    return low_back(low(value))

def matmul(left, right):
    return jnp.matmul(left, right, precision=lax.Precision.HIGHEST)

def norm_rows(values, gains, shifts):
    centre = lax.optimization_barrier(jnp.mean(values, axis=-1, keepdims=True))
    offset = values - centre
    spread = lax.optimization_barrier(jnp.mean(offset * offset, axis=-1, keepdims=True))
    return offset * lax.rsqrt(spread + 1e-05) * gains + shifts

def segment_ids(lengths, count):
    bounds = jnp.cumsum(lengths, axis=-1)
    positions = jnp.arange(count, dtype=jnp.int32)
    return lax.optimization_barrier(jnp.sum((positions[None, :, None] >= bounds[:, None, :]).astype(jnp.int32), axis=-1)).astype(jnp.int32)

def split_heads(values):
    return values.reshape(values.shape[:-1] + (HEADS, HEAD_DIM))

def softmax_rows(scores):
    peak = lax.optimization_barrier(jnp.max(scores, axis=-1, keepdims=True))
    weights = jnp.exp(scores - peak)
    return weights / lax.optimization_barrier(jnp.sum(weights, axis=-1, keepdims=True))

def gelu_tanh(values):
    return jax.nn.gelu(values, approximate=True)

def block_forward(params, tokens, memory, self_mask, cross_mask):
    attention_in, attention_out, attention_bias, gains, shifts, expand_weight, expand_bias, reduce_weight, reduce_bias = params
    factor = 1.0 / math.sqrt(HEAD_DIM)
    highest = lax.Precision.HIGHEST
    normed = low(norm_rows(tokens, gains[0], shifts[0]))
    queries = both_ways(matmul(normed, attention_in[0, 0]) + attention_bias[0, 0])
    key_rows = both_ways(matmul(normed, attention_in[0, 1]))
    value_rows = both_ways(matmul(normed, attention_in[0, 2]) + attention_bias[0, 1])
    scores = low_back(jnp.einsum('aqhd,akhd->ahqk', split_heads(queries), split_heads(key_rows), precision=highest) * factor)
    weights = softmax_rows(jnp.where(self_mask[:, None], scores, -1e+30))
    context = jnp.einsum('ahqk,akhd->aqhd', low(weights), split_heads(value_rows), precision=highest)
    context = both_ways(context.reshape(tokens.shape))
    after_self = tokens + low_back(matmul(context, attention_out[0]) + attention_bias[0, 2])
    normed = low(norm_rows(after_self, gains[1], shifts[1]))
    queries = both_ways(matmul(normed, attention_in[1, 0]) + attention_bias[1, 0])
    key_rows = both_ways(matmul(memory, attention_in[1, 1]))
    value_rows = both_ways(matmul(memory, attention_in[1, 2]) + attention_bias[1, 1])
    scores = low_back(jnp.einsum('aqhd,akhd->ahqk', split_heads(queries), split_heads(key_rows), precision=highest) * factor)
    weights = softmax_rows(jnp.where(cross_mask[:, None], scores, -1e+30))
    context = jnp.einsum('ahqk,akhd->aqhd', weights, split_heads(value_rows), precision=highest)
    context = both_ways(context.reshape(tokens.shape))
    after_cross = after_self + low_back(matmul(context, attention_out[1]) + attention_bias[1, 2])
    normed = low(norm_rows(after_cross, gains[2], shifts[2]))
    inner_act = low_back(matmul(normed, expand_weight) + expand_bias)
    active = low(gelu_tanh(inner_act))
    after_ffn = after_cross + low_back(matmul(active, reduce_weight) + reduce_bias)
    return norm_rows(after_ffn, gains[3], shifts[3])

def reference(tokens, memory, token_lengths, frame_lengths, attention_in, attention_out, attention_bias, norm_gain, norm_bias, expand_weight, expand_bias, reduce_weight, reduce_bias, cotangent):
    params = tuple((item.astype(jnp.float32) for item in (attention_in, attention_out, attention_bias, norm_gain, norm_bias, expand_weight, expand_bias, reduce_weight, reduce_bias)))
    groups = MB * PAIRS
    flat_tokens = tokens.reshape(groups, HALVES, ROWS, D)
    flat_memory = memory.reshape(groups, HALVES, MEM, D)
    flat_cot = cotangent.reshape(groups, HALVES, ROWS, D)
    flat_token_len = token_lengths.reshape(groups, HALVES, NSEQ)
    flat_frame_len = frame_lengths.reshape(groups, HALVES, NSEQ)
    positions = jnp.arange(ROWS, dtype=jnp.int32)
    causal = positions[None, :] <= positions[:, None]

    def group_step(totals, inputs):
        piece_tokens, piece_memory, piece_cot, token_len, frame_len = inputs
        token_seg = segment_ids(token_len, ROWS)
        frame_seg = segment_ids(frame_len, MEM)
        self_mask = (token_seg[:, :, None] == token_seg[:, None, :]) & causal[None]
        cross_mask = token_seg[:, :, None] == frame_seg[:, None, :]

        def forward(weights, inputs_tokens, inputs_memory):
            return block_forward(weights, inputs_tokens, inputs_memory, self_mask, cross_mask)
        output, pullback = jax.vjp(forward, params, piece_tokens.astype(jnp.float32), piece_memory.astype(jnp.float32))
        grad_params, grad_tokens, grad_memory = pullback(piece_cot.astype(jnp.float32))
        totals = jax.tree.map(jnp.add, totals, grad_params)
        return (totals, (output.astype(jnp.bfloat16), grad_tokens, grad_memory))
    zeros = tuple((jnp.zeros(item.shape, jnp.float32) for item in params))
    totals, results = lax.scan(group_step, zeros, (flat_tokens, flat_memory, flat_cot, flat_token_len, flat_frame_len))
    outputs, grad_tokens, grad_memory = results
    return (outputs.reshape(tokens.shape), grad_tokens.reshape(tokens.shape), grad_memory.reshape(memory.shape), totals[0], totals[1], totals[2], totals[3], totals[4], totals[5], totals[6], totals[7], totals[8])
```

```python
import functools
import math

import jax
import jax.numpy as jnp
import numpy as np
from jax import lax
from jax.experimental import pallas as pl
from jax.experimental.pallas import tpu as pltpu
from jax.sharding import PartitionSpec as P

D = 1024
HEADS = 16
HEAD_DIM = 64
FACTOR = 1.0 / math.sqrt(HEAD_DIM)
BF = jnp.bfloat16
F32 = jnp.float32


def dot(a, b):
    return jnp.dot(a, b, preferred_element_type=F32)


def dot_t(a, b):
    return lax.dot_general(a, b, (((1,), (1,)), ((), ())), preferred_element_type=F32)


def norm_stats(v):
    centre = jnp.mean(v, axis=-1, keepdims=True)
    off = v - centre
    r = lax.rsqrt(jnp.mean(off * off, axis=-1, keepdims=True) + 1e-5)
    return off * r, r


def norm_back(e, n, r, gain):
    eg = e * gain
    return r * (
        eg - jnp.mean(eg, axis=-1, keepdims=True) - n * jnp.mean(eg * n, axis=-1, keepdims=True)
    )


def segment_ids(lengths, count):
    bounds = jnp.cumsum(lengths, axis=-1)
    positions = jnp.arange(count, dtype=jnp.int32)
    return jnp.sum((positions[None, :, None] >= bounds[:, None, :]).astype(jnp.int32), axis=-1)


def heads(x, nb):
    return x.reshape(nb, -1, HEADS, HEAD_DIM)


def stage_bits(n_dp):
    m = n_dp.bit_length() - 1
    if m == 4:
        return [[0, 2, 1, 3], [1, 2, 0, 3]]
    evens = [b for b in range(m) if b % 2 == 0]
    odds = [b for b in range(m) if b % 2 == 1]
    one = evens + odds
    two = evens[1:] + evens[:1] + odds[1:] + odds[:1]
    return [one, two]


def place_table(n_dp):
    bits = stage_bits(n_dp)
    n = 2 * n_dp
    m = len(bits[0])
    table = np.zeros((2, n), np.int32)
    for f in range(2):
        for p in range(n):
            far = p >> m
            order = bits[1 - f] if far else bits[f]
            mask = far
            for s in range(m):
                if (p >> (m - 1 - s)) & 1:
                    mask ^= 2 << order[s]
            table[f, p] = mask
    return table


def core_pairs(n_dp):
    return [(d * 2 + f, d * 2 + 1 - f) for d in range(n_dp) for f in range(2)]


def stage_pairs(n_dp, s):
    bits = stage_bits(n_dp)
    return [(d * 2 + f, (d ^ (1 << bits[f][s])) * 2 + f) for d in range(n_dp) for f in range(2)]


AXES = ("dp", "frame")


def permute(x, pairs):
    return lax.ppermute(x, AXES, pairs)


def grad_kernel(half, n_half, r, with_add, table_ref, at_ref, b_ref, *rest):
    if with_add:
        add_ref, send_ref, keep_ref, perm = rest
    else:
        send_ref, perm = rest

    @pl.when(pl.program_id(0) == 0)
    def _():
        for p in range(n_half):
            src = table_ref[half * n_half + p]
            perm[pl.ds(p * r, r), :] = at_ref[pl.ds(pl.multiple_of(src * r, r), r), :]

    rows = n_half * r
    step = min(rows, 512)
    for i in range(rows // step):
        out = dot(perm[pl.ds(i * step, step), :], b_ref[...])
        if not with_add:
            send_ref[pl.ds(i * step, step), :] = out.astype(BF)
        else:
            out = (out + add_ref[pl.ds(i * step, step), :].astype(F32)).astype(BF)
            edge = rows // 2
            lo, hi = i * step, (i + 1) * step
            if lo < edge:
                cut = min(hi, edge)
                keep_ref[pl.ds(lo, cut - lo), :] = out[: cut - lo]
            if hi > edge:
                start = max(lo, edge)
                send_ref[pl.ds(start - edge, hi - start), :] = out[start - lo :]


def grad_half(table, at, b, n, half, add=None):
    feats, rows = at.shape
    cols = b.shape[1]
    r = feats // n
    n_half = n // 2
    tile = min(cols, 512)
    m = n_half * r
    with_add = add is not None
    col = lambda i, t: (0, i)
    in_specs = [pl.BlockSpec((feats, rows), lambda i, t: (0, 0)), pl.BlockSpec((rows, tile), col)]
    args = [at, b]
    if with_add:
        in_specs.append(pl.BlockSpec((m, tile), col))
        args.append(add)
        out_shape = [jax.ShapeDtypeStruct((m // 2, cols), BF)] * 2
        out_specs = [pl.BlockSpec((m // 2, tile), col)] * 2
    else:
        out_shape = jax.ShapeDtypeStruct((m, cols), BF)
        out_specs = pl.BlockSpec((m, tile), col)
    return pl.pallas_call(
        functools.partial(grad_kernel, half, n_half, r, with_add),
        out_shape=out_shape,
        grid_spec=pltpu.PrefetchScalarGridSpec(
            num_scalar_prefetch=1,
            grid=(cols // tile,),
            in_specs=in_specs,
            out_specs=out_specs,
            scratch_shapes=[pltpu.VMEM((m, rows), BF)],
        ),
        compiler_params=pltpu.CompilerParams(vmem_limit_bytes=40 * 2**20),
        cost_estimate=pl.CostEstimate(
            flops=2 * m * rows * cols,
            bytes_accessed=2 * (feats * rows + rows * cols + m * cols * (2 if with_add else 1)),
            transcendentals=0,
        ),
    )(table, at, b, *args[2:])


def halve(send, keep, n_dp, first):
    stages = n_dp.bit_length() - 1
    for s in range(first, stages):
        got = permute(send, stage_pairs(n_dp, s))
        total = keep.astype(F32) + got.astype(F32)
        if s == stages - 1:
            return total
        total = total.astype(send.dtype)
        edge = total.shape[0] // 2
        keep, send = total[:edge], total[edge:]
    return keep


def scatter_grad(table, at, b, n):
    n_dp = n // 2
    far = grad_half(table, at, b, n, 1)
    got = permute(far, core_pairs(n_dp))
    send, keep = grad_half(table, at, b, n, 0, got)
    return halve(send, keep, n_dp, 0)


def scatter_small(packed, table, n):
    n_dp = n // 2
    placed = jnp.take(packed, table, axis=0)
    edge = n // 2
    near = placed[:edge] + permute(placed[edge:], core_pairs(n_dp))
    return halve(near[edge // 2 :], near[: edge // 2], n_dp, 0)


def col_sum(v):
    return jnp.sum(v.astype(F32), axis=0)


def local(
    n_dp,
    tokens,
    memory,
    token_lengths,
    frame_lengths,
    attention_in,
    attention_out,
    attention_bias,
    norm_gain,
    norm_bias,
    expand_weight,
    expand_bias,
    reduce_weight,
    reduce_bias,
    cotangent,
):
    n = 2 * n_dp
    frame = lax.axis_index("frame")
    me = lax.axis_index("dp") * 2 + frame
    table = jnp.bitwise_xor(me, jnp.asarray(place_table(n_dp))[frame]).astype(jnp.int32)
    nb, rows = tokens.shape[0], tokens.shape[3]
    half = memory.shape[3]
    frames = 2 * half
    total_rows = nb * rows

    own_mem = lax.dynamic_index_in_dim(memory[:, 0], frame, 1, False)
    far_mem = lax.dynamic_index_in_dim(memory[:, 0], 1 - frame, 1, False)
    mem = jnp.concatenate([own_mem, permute(far_mem, core_pairs(n_dp))], axis=1)
    mem = mem.reshape(nb * frames, D)

    tok_len = lax.dynamic_index_in_dim(token_lengths[:, 0], frame, 1, False)
    frm_len = lax.dynamic_index_in_dim(frame_lengths[:, 0], frame, 1, False)
    tok_seg = segment_ids(tok_len, rows)
    frm_seg = segment_ids(frm_len, frames)
    frm_seg = jnp.where(frame == 0, frm_seg, jnp.roll(frm_seg, -half, axis=1))
    pos = jnp.arange(rows, dtype=jnp.int32)
    self_mask = (tok_seg[:, :, None] == tok_seg[:, None, :]) & (pos[None, :] <= pos[:, None])[None]
    cross_mask = tok_seg[:, :, None] == frm_seg[:, None, :]

    def attend(q, k, v, mask):
        s = jnp.einsum(
            "bqhd,bkhd->bhqk", heads(q, nb), heads(k, nb), preferred_element_type=F32
        ) * FACTOR
        s = jnp.where(mask[:, None], s, -1e30)
        e = jnp.exp(s - jnp.max(s, axis=-1, keepdims=True))
        p = (e / jnp.sum(e, axis=-1, keepdims=True)).astype(BF)
        c = jnp.einsum("bhqk,bkhd->bqhd", p, heads(v, nb), preferred_element_type=F32)
        return p, c.reshape(total_rows, D).astype(BF)

    def attend_back(p, q, k, v, dc):
        dch = heads(dc, nb)
        dp = jnp.einsum("bqhd,bkhd->bhqk", dch, heads(v, nb), preferred_element_type=F32)
        pf = p.astype(F32)
        ds = (pf * (dp - jnp.sum(dp * pf, axis=-1, keepdims=True))).astype(BF)
        dq = jnp.einsum("bhqk,bkhd->bqhd", ds, heads(k, nb), preferred_element_type=F32) * FACTOR
        dk = jnp.einsum("bhqk,bqhd->bkhd", ds, heads(q, nb), preferred_element_type=F32) * FACTOR
        dv = jnp.einsum("bhqk,bqhd->bkhd", p, dch, preferred_element_type=F32)
        return [x.reshape(-1, D).astype(BF) for x in (dq, dk, dv)]

    w_in, w_out, bias = attention_in, attention_out, attention_bias
    h = tokens.reshape(total_rows, D).astype(F32)
    n0, r0 = norm_stats(h)
    a0 = (n0 * norm_gain[0] + norm_bias[0]).astype(BF)
    q = (dot(a0, w_in[0, 0]) + bias[0, 0]).astype(BF)
    k = dot(a0, w_in[0, 1]).astype(BF)
    v = (dot(a0, w_in[0, 2]) + bias[0, 1]).astype(BF)
    p, c = attend(q, k, v, self_mask)
    h1 = h + dot(c, w_out[0]) + bias[0, 2]
    n1, r1 = norm_stats(h1)
    a1 = (n1 * norm_gain[1] + norm_bias[1]).astype(BF)
    cq = (dot(a1, w_in[1, 0]) + bias[1, 0]).astype(BF)
    ck = dot(mem, w_in[1, 1]).astype(BF)
    cv = (dot(mem, w_in[1, 2]) + bias[1, 1]).astype(BF)
    cp, cc = attend(cq, ck, cv, cross_mask)
    h2 = h1 + dot(cc, w_out[1]) + bias[1, 2]
    n2, r2 = norm_stats(h2)
    a2 = (n2 * norm_gain[2] + norm_bias[2]).astype(BF)
    u = dot(a2, expand_weight) + expand_bias
    g, pull_act = jax.vjp(lambda x: jax.nn.gelu(x, approximate=True), u)
    g = g.astype(BF)
    h3 = h2 + dot(g, reduce_weight) + reduce_bias
    n3, r3 = norm_stats(h3)
    out = (n3 * norm_gain[3] + norm_bias[3]).astype(BF)
    e3 = cotangent.reshape(total_rows, D).astype(F32)
    dh3 = norm_back(e3, n3, r3, norm_gain[3])
    df = dh3.astype(BF)
    half_cols = D // 2
    gT = g.T
    grad_reduce = [
        scatter_grad(table, gT, df[:, i * half_cols : (i + 1) * half_cols], n) for i in range(2)
    ]
    du = pull_act(dot_t(df, reduce_weight))[0].astype(BF)
    ff = expand_weight.shape[1]
    a2T = a2.T
    grad_expand = [
        scatter_grad(table, a2T, du[:, i * ff // 2 : (i + 1) * ff // 2], n) for i in range(2)
    ]
    e2 = dot_t(du, expand_weight)
    dh2 = dh3 + norm_back(e2, n2, r2, norm_gain[2])
    dx2 = dh2.astype(BF)
    grad_out1 = scatter_grad(table, cc.T, dx2, n)
    dcc = dot_t(dx2, w_out[1]).astype(BF)
    dcq, dck, dcv = attend_back(cp, cq, ck, cv, dcc)
    grad_q1 = scatter_grad(table, a1.T, dcq, n)
    dckv = jnp.concatenate([dck, dcv], axis=1)
    grad_kv1 = scatter_grad(table, mem.T, dckv, n)
    e1 = dot_t(dcq, w_in[1, 0])
    grad_mem = (dot_t(dck, w_in[1, 1]) + dot_t(dcv, w_in[1, 2])).reshape(nb, frames, D)
    own_gm = grad_mem[:, :half]
    far_gm = permute(grad_mem[:, half:], core_pairs(n_dp))
    grad_memory = jnp.where(
        frame == 0, jnp.stack([own_gm, far_gm], axis=1), jnp.stack([far_gm, own_gm], axis=1)
    )[:, None]
    dh1 = dh2 + norm_back(e1, n1, r1, norm_gain[1])
    dx1 = dh1.astype(BF)
    grad_out0 = scatter_grad(table, c.T, dx1, n)
    dc = dot_t(dx1, w_out[0]).astype(BF)
    dq, dk, dv = attend_back(p, q, k, v, dc)
    dqkv = jnp.concatenate([dq, dk, dv], axis=1)
    grad_qkv0 = scatter_grad(table, a0.T, dqkv, n)
    e0 = dot_t(dq, w_in[0, 0]) + dot_t(dk, w_in[0, 1]) + dot_t(dv, w_in[0, 2])
    grad_tokens = dh1 + norm_back(e0, n0, r0, norm_gain[0])

    small = jnp.concatenate(
        [
            x.reshape(n, -1)
            for x in (
                col_sum(dq), col_sum(dv), col_sum(dx1), col_sum(dcq), col_sum(dcv), col_sum(dx2),
                col_sum(e0 * n0), col_sum(e1 * n1), col_sum(e2 * n2), col_sum(e3 * n3),
                col_sum(e0), col_sum(e1), col_sum(e2), col_sum(e3),
                col_sum(du), col_sum(df),
            )
        ],
        axis=1,
    )
    small = scatter_small(small, table, n)[0]
    w = D // n
    grad_bias = small[: 6 * w].reshape(2, 3, w)
    grad_gain = small[6 * w : 10 * w].reshape(4, w)
    grad_shift = small[10 * w : 14 * w].reshape(4, w)
    wide = ff // n
    grad_eb = small[14 * w : 14 * w + wide]
    grad_rb = small[14 * w + wide :]

    kv = jnp.split(grad_kv1, 2, axis=1)
    qkv = jnp.split(grad_qkv0, 3, axis=1)
    grad_in = jnp.stack([jnp.stack(qkv), jnp.stack([grad_q1] + kv)])
    grad_out = jnp.stack([grad_out0, grad_out1])
    shape = tokens.shape
    return (
        out.reshape(shape),
        grad_tokens.reshape(shape),
        grad_memory,
        grad_in,
        grad_out,
        grad_bias,
        grad_gain,
        grad_shift,
        jnp.concatenate(grad_expand, axis=1),
        grad_eb,
        jnp.concatenate(grad_reduce, axis=1),
        grad_rb,
    )


def solution(mesh):
    spread = P(None, "dp", "frame", None, None)
    by_frame = P(None, "dp", None, "frame", None)
    both = ("dp", "frame")
    lengths = P(None, "dp", None, None)
    return jax.shard_map(
        functools.partial(local, mesh.shape["dp"]),
        mesh=mesh,
        in_specs=(spread, by_frame, lengths, lengths) + (P(),) * 9 + (spread,),
        out_specs=(
            spread,
            spread,
            by_frame,
            P(None, None, both, None),
            P(None, both, None),
            P(None, None, both),
            P(None, both),
            P(None, both),
            P(both, None),
            P(both),
            P(both, None),
            P(both),
        ),
        check_vma=False,
    )
```

```python
import functools
import math

import jax
import jax.numpy as jnp
from jax import lax
from jax.experimental import pallas as pl
from jax.experimental.pallas import tpu as pltpu
from jax.sharding import PartitionSpec as P

D = 1024
HEADS = 16
HEAD_DIM = 64
FACTOR = 1.0 / math.sqrt(HEAD_DIM)
BF = jnp.bfloat16
F32 = jnp.float32


def dot(a, b):
    return jnp.dot(a, b, preferred_element_type=F32)


def dot_t(a, b):
    return lax.dot_general(a, b, (((1,), (1,)), ((), ())), preferred_element_type=F32)


def core_pairs(n_dp):
    return [(d * 2 + f, d * 2 + 1 - f) for d in range(n_dp) for f in range(2)]


AXES = ("dp", "frame")


def permute(x, pairs):
    return lax.ppermute(x, AXES, pairs)


VM = pl.BlockSpec(memory_space=pltpu.VMEM)
SM = pl.BlockSpec(memory_space=pltpu.SMEM)
ANY = pl.BlockSpec(memory_space=pl.ANY)
GELU_C = 0.7978845608028654
GELU_D = 0.044715 * GELU_C


def params(mib=58):
    return pltpu.CompilerParams(vmem_limit_bytes=mib * 2**20)


def cost(flops, nbytes, trans=0):
    return pl.CostEstimate(flops=1, bytes_accessed=1, transcendentals=0)


def hbm(shape, kind):
    return jax.ShapeDtypeStruct(shape, kind)


class Copies:
    def __init__(self, sems):
        self.sems, self.copies, self.done = sems, [], 0

    def start(self, *pairs):
        for src, dst in pairs:
            copy = pltpu.make_async_copy(src, dst, self.sems.at[len(self.copies)])
            copy.start()
            self.copies.append(copy)

    def wait(self, count=1):
        for copy in self.copies[self.done : self.done + count]:
            copy.wait()
        self.done += count

    def wait_all(self):
        self.wait(len(self.copies) - self.done)


def stats(v):
    off = v - jnp.mean(v, axis=-1, keepdims=True)
    r = lax.rsqrt(jnp.mean(off * off, axis=-1, keepdims=True) + 1e-5)
    return off * r, r


def norm_back(e, v, gain):
    n, r = stats(v)
    eg = e * gain
    back = r * (
        eg - jnp.mean(eg, axis=-1, keepdims=True) - n * jnp.mean(eg * n, axis=-1, keepdims=True)
    )
    return back, row_sum(e * n), row_sum(e)


def row_sum(x):
    return jnp.sum(x.astype(F32), axis=0, keepdims=True)


def pair_mask(rows):
    return lax.broadcasted_iota(jnp.int32, (rows, 128), 1) < HEAD_DIM


def segments(lengths, b, a, shape, dim, shift=0):
    pos = lax.broadcasted_iota(jnp.int32, shape, dim) + shift
    pos = jnp.where(pos >= shape[dim], pos - shape[dim], pos)
    total, seg = 0, jnp.zeros(shape, jnp.int32)
    for i in range(lengths.shape[3] - 1):
        total = total + lengths[b, 0, a, i]
        seg = seg + (pos >= total).astype(jnp.int32)
    return seg


def attend(nb, rows, cols, q, k, v, e_ref, r_ref, c, mask, unroll=4):
    low = pair_mask(rows)
    one = jnp.ones((cols, 128), BF)

    def pair(j, _):
        lanes = pl.ds(pl.multiple_of(j * 128, 128), 128)
        for b in range(nb):
            qs, ks = pl.ds(b * rows, rows), pl.ds(b * cols, cols)
            q2, k2, v2 = q[qs, lanes], k[ks, lanes], v[ks, lanes]
            zero = jnp.zeros_like(q2)
            both = jnp.concatenate([jnp.where(low, q2, zero), jnp.where(low, zero, q2)], axis=0)
            s = dot_t(both, k2).reshape(2, rows, cols) + mask[b][None]
            e = jnp.exp(s - jnp.max(s, axis=-1, keepdims=True)).astype(BF)
            e_ref[b, pl.ds(2 * j, 2)] = e
            o = dot(e.reshape(2 * rows, cols), jnp.concatenate([v2, one], axis=1))
            r = 1.0 / jnp.where(low, o[:rows, 128:], o[rows:, 128:])
            r_ref[qs, lanes] = r
            c[qs, lanes] = (jnp.where(low, o[:rows, :128], o[rows:, :128]) * r).astype(BF)
        return 0

    lax.fori_loop(0, HEADS // 2, pair, 0, unroll=unroll)


def attend_back(nb, rows, cols, part, e_ref, r_ref, q, k, v, c, dc, dq, dk, dv):
    low, low_k = pair_mask(rows), pair_mask(cols)
    minus = jnp.full((cols, 128), -1, BF)

    count = HEADS // 2 // PARTS
    for j in range(part * count, (part + 1) * count):
        lanes = pl.ds(j * 128, 128)
        for b in range(nb):
            qs, ks = pl.ds(b * rows, rows), pl.ds(b * cols, cols)
            q2, k2, v2 = q[qs, lanes], k[ks, lanes], v[ks, lanes]
            dcs = dc[qs, lanes].astype(F32) * r_ref[qs, lanes]
            delta = (dcs * c[qs, lanes].astype(F32)).astype(BF)
            dcs = dcs.astype(BF)
            zero = jnp.zeros_like(dcs)
            first = jnp.concatenate([jnp.where(low, dcs, zero), jnp.where(low, delta, zero)], axis=1)
            second = jnp.concatenate([jnp.where(low, zero, dcs), jnp.where(low, zero, delta)], axis=1)
            slope = dot_t(
                jnp.concatenate([first, second], axis=0), jnp.concatenate([v2, minus], axis=1)
            )
            e = e_ref[b, pl.ds(2 * j, 2)]
            ds = (e.astype(F32) * slope.reshape(2, rows, cols)).astype(BF)
            g = dot(ds.reshape(2 * rows, cols), k2)
            dq[qs, lanes] = (jnp.where(low, g[:rows], g[rows:]) * FACTOR).astype(BF)
            g = dot(jnp.concatenate([ds[0].T, ds[1].T], axis=0), q2)
            dk[ks, lanes] = jnp.where(low_k, g[:cols], g[cols:]).astype(BF)
            g = dot(jnp.concatenate([e[0].T, e[1].T], axis=0), dcs)
            dv[ks, lanes] = jnp.where(low_k, g[:cols], g[cols:]).astype(BF)


def self_kernel(
    nb, lengths, bias, gain, shift, tok_h, w_in, w_out,
    q_o, k_o, v_o, e_o, r_o, c_o, h1_o, a0_o, a1_o, cq_o,
    tok, wbuf, a0, q, k, v, e, r, c, h1, a1, cq, mask, lsem, ssem,
):
    rows = tok.shape[0] // nb
    frame = lax.axis_index("frame")
    loads, stores = Copies(lsem), Copies(ssem)
    loads.start((tok_h, tok))
    mats = [w_in.at[0, 0], w_in.at[0, 1], w_in.at[0, 2], w_out.at[0], w_in.at[1, 0]]
    loads.start(*[(m, wbuf.at[i]) for i, m in enumerate(mats)])
    square = (rows, rows)
    causal = lax.broadcasted_iota(jnp.int32, square, 1) <= lax.broadcasted_iota(jnp.int32, square, 0)
    for b in range(nb):
        same = segments(lengths, b, frame, square, 0) == segments(lengths, b, frame, square, 1)
        mask[b] = jnp.where(same & causal, 0.0, -1e30)
    loads.wait()
    n0, _ = stats(tok[...].astype(F32))
    a0[...] = (n0 * gain[0:1, :] + shift[0:1, :]).astype(BF)
    loads.wait()
    q[...] = ((dot(a0[...], wbuf[0]) + bias[0:1, :]).astype(BF).astype(F32) * FACTOR).astype(BF)
    loads.wait()
    k[...] = dot(a0[...], wbuf[1]).astype(BF)
    loads.wait()
    v[...] = (dot(a0[...], wbuf[2]) + bias[1:2, :]).astype(BF)
    stores.start((a0, a0_o), (q, q_o), (k, k_o), (v, v_o))
    attend(nb, rows, rows, q, k, v, e, r, c, mask)
    stores.start((e, e_o), (r, r_o), (c, c_o))
    loads.wait()
    h1[...] = tok[...].astype(F32) + dot(c[...], wbuf[3]) + bias[2:3, :]
    n1, _ = stats(h1[...])
    a1[...] = (n1 * gain[1:2, :] + shift[1:2, :]).astype(BF)
    stores.start((h1, h1_o), (a1, a1_o))
    loads.wait()
    cq[...] = ((dot(a1[...], wbuf[4]) + bias[3:4, :]).astype(BF).astype(F32) * FACTOR).astype(BF)
    stores.start((cq, cq_o))
    stores.wait_all()


def self_forward(nb, lengths, bias, gain, shift, tok, w_in, w_out):
    t, d = tok.shape
    rows = t // nb
    act = (t, d)
    eshape = (nb, HEADS, rows, rows)
    kinds = [(act, BF)] * 3 + [(eshape, BF), (act, F32), (act, BF), (act, F32)] + [(act, BF)] * 3
    order = [7, 0, 1, 2, 3, 4, 5, 6, 8, 9]
    return pl.pallas_call(
        functools.partial(self_kernel, nb),
        out_shape=[hbm(*x) for x in kinds],
        in_specs=[SM, VM, VM, VM, ANY, ANY, ANY],
        out_specs=[ANY] * 10,
        scratch_shapes=[
            pltpu.VMEM(act, BF),
            pltpu.VMEM((5, d, d), BF),
            *[pltpu.VMEM(*kinds[i]) for i in order],
            pltpu.VMEM((nb, rows, rows), F32),
            pltpu.SemaphoreType.DMA((6,)),
            pltpu.SemaphoreType.DMA((10,)),
        ],
        compiler_params=params(),
        cost_estimate=cost(12 * t * d * d, 12e6 * 2, 1e6),
        name="self_forward",
    )(lengths, bias, gain, shift, tok, w_in, w_out)


def rest_kernel(
    nb, steps, tok_len, frm_len, bias, gain, shift, rb, eb,
    memory, far, cq_h, h1_h, cot_h, w_in, w_out, we, wr,
    mem_o, k_o, v_o, e_o, r_o, c_o, h2_o, a2_o, u_o, g_o, out_o, dh3_o, df_o, sums_o,
    mem, cq, h1, cot, wbuf, webuf, wrbuf, k, v, e, r, c, h2, a2, u, g, acc, out, df, mask, lsem, ssem,
):
    rows, cols = h1.shape[0] // nb, mem.shape[0] // nb
    half = cols // 2
    tile = webuf.shape[2]
    frame = lax.axis_index("frame")
    loads, stores = Copies(lsem), Copies(ssem)
    for b in range(nb):
        loads.start(
            (memory.at[b, 0, frame], mem.at[pl.ds(b * cols, half)]),
            (far.at[b, 0, frame], mem.at[pl.ds(b * cols + half, half)]),
        )
    loads.start((w_in.at[1, 1], wbuf.at[0]), (w_in.at[1, 2], wbuf.at[1]))
    loads.start((cq_h, cq), (w_out.at[1], wbuf.at[2]), (h1_h, h1))
    for j in range(steps):
        loads.start((we.at[:, pl.ds(j * tile, tile)], webuf.at[j]), (wr.at[pl.ds(j * tile, tile)], wrbuf.at[j]))
    loads.start((cot_h, cot))
    shape = (rows, cols)
    for b in range(nb):
        same = segments(tok_len, b, frame, shape, 0) == segments(frm_len, b, frame, shape, 1, frame * half)
        mask[b] = jnp.where(same, 0.0, -1e30)
    loads.wait(2 * nb + 1)
    stores.start((mem, mem_o))
    k[...] = dot(mem[...], wbuf[0]).astype(BF)
    loads.wait()
    v[...] = (dot(mem[...], wbuf[1]) + bias[4:5, :]).astype(BF)
    stores.start((k, k_o), (v, v_o))
    loads.wait()
    attend(nb, rows, cols, cq, k, v, e, r, c, mask)
    stores.start((e, e_o), (r, r_o), (c, c_o))
    loads.wait(2)
    h2[...] = h1[...] + dot(c[...], wbuf[2]) + bias[5:6, :]
    n2, _ = stats(h2[...])
    a2[...] = (n2 * gain[2:3, :] + shift[2:3, :]).astype(BF)
    stores.start((h2, h2_o), (a2, a2_o))
    for j in range(steps + 1):
        if j < steps:
            loads.wait(2)
        if j > 0:
            stores.start((u.at[j - 1], u_o.at[j - 1]), (g.at[j - 1], g_o.at[:, pl.ds((j - 1) * tile, tile)]))
        if j < steps:
            x = dot(a2[...], webuf[j]) + eb[:, j * tile : (j + 1) * tile]
            u[j] = x.astype(BF)
            g[j] = (0.5 * x * (1.0 + jnp.tanh(x * (GELU_C + GELU_D * (x * x))))).astype(BF)
        if j == 1:
            acc[...] = (h2[...] + rb[...]) + dot(g[0], wrbuf[0])
        elif j > 1:
            acc[...] += dot(g[j - 1], wrbuf[j - 1])
    loads.wait()
    n3, r3 = stats(acc[...])
    out[...] = (n3 * gain[3:4, :] + shift[3:4, :]).astype(BF)
    stores.start((out, out_o))
    up = cot[...].astype(F32)
    sums_o[0:1, :] = row_sum(up * n3)
    sums_o[1:2, :] = row_sum(up)
    eg = up * gain[3:4, :]
    back = r3 * (
        eg - jnp.mean(eg, axis=-1, keepdims=True) - n3 * jnp.mean(eg * n3, axis=-1, keepdims=True)
    )
    acc[...] = back
    low = back.astype(BF)
    df[...] = low
    stores.start((df, df_o), (acc, dh3_o))
    sums_o[2:3, :] = row_sum(low)
    stores.wait_all()


def rest_forward(
    nb, tok_len, frm_len, bias, gain, shift, rb, eb, memory, far, cq, h1, cot, w_in, w_out, we, wr, tile=512
):
    t, d = h1.shape
    ff = we.shape[1]
    steps = ff // tile
    m = 2 * nb * memory.shape[3]
    rows, cols = t // nb, m // nb
    act, macts = (t, d), (m, d)
    eshape = (nb, HEADS, rows, cols)
    ushape = (steps, t, tile)
    sem = pltpu.SemaphoreType.DMA
    return pl.pallas_call(
        functools.partial(rest_kernel, nb, steps),
        out_shape=[
            hbm(macts, BF), hbm(macts, BF), hbm(macts, BF), hbm(eshape, BF), hbm(act, F32), hbm(act, BF),
            hbm(act, F32), hbm(act, BF), hbm(ushape, BF), hbm((t, ff), BF), hbm(act, BF), hbm(act, F32),
            hbm(act, BF), hbm((8, d), F32),
        ],
        in_specs=[SM] * 2 + [VM] * 5 + [ANY] * 9,
        out_specs=[ANY] * 13 + [VM],
        scratch_shapes=[
            pltpu.VMEM(macts, BF),
            pltpu.VMEM(act, BF),
            pltpu.VMEM(act, F32),
            pltpu.VMEM(act, BF),
            pltpu.VMEM((3, d, d), BF),
            pltpu.VMEM((steps, d, tile), BF),
            pltpu.VMEM((steps, tile, d), BF),
            pltpu.VMEM(macts, BF),
            pltpu.VMEM(macts, BF),
            pltpu.VMEM(eshape, BF),
            pltpu.VMEM(act, F32),
            pltpu.VMEM(act, BF),
            pltpu.VMEM(act, F32),
            pltpu.VMEM(act, BF),
            pltpu.VMEM(ushape, BF),
            pltpu.VMEM(ushape, BF),
            pltpu.VMEM(act, F32),
            pltpu.VMEM(act, BF),
            pltpu.VMEM(act, BF),
            pltpu.VMEM((nb, rows, cols), F32),
            sem((2 * nb + 6 + 2 * steps,)),
            sem((11 + 2 * steps,)),
        ],
        compiler_params=params(),
        cost_estimate=cost(6 * t * d * d + 4 * t * d * ff, 30e6, 3e6),
        name="rest_forward",
    )(tok_len, frm_len, bias, gain, shift, rb, eb, memory, far, cq, h1, cot, w_in, w_out, we, wr)


PARTS = 4


def start_parts(loads, nb, e_h, e, *pairs):
    for i in range(PARTS):
        heads = pl.ds(i * HEADS // PARTS, HEADS // PARTS)
        loads.start((e_h.at[:, heads], e.at[:, heads]))
        for src, dst in pairs:
            lanes = pl.ds(i * (D // PARTS), D // PARTS)
            loads.start((src.at[:, lanes], dst.at[:, lanes]))


K_SLOTS = 10
R_SLOTS = 6
S_SLOTS = 4
C_SLOTS = 6
F_SLOTS = 4
PERIOD = 7.0
START = 5.0


def stage_masks(n_dp):
    m = n_dp.bit_length() - 1
    if m == 4:
        orders = [0, 2, 1, 3], [1, 2, 0, 3]
    else:
        one = list(range(0, m, 2)) + list(range(1, m, 2))
        orders = one, one[1:] + one[:1]
    return [(1 << a, 1 << b) for a, b in zip(*orders)]


def place_masks(n_dp):
    masks = stage_masks(n_dp)
    m = len(masks)
    out = []
    for f in range(2):
        row = []
        for p in range(2 * n_dp):
            far = p >> m
            mask = far
            for s in range(m):
                if (p >> (m - 1 - s)) & 1:
                    mask ^= 2 * masks[s][1 - f if far else f]
            row.append(mask)
        out.append(row)
    return out


def shard_at(n_dp, dp, frame, p):
    masks = place_masks(n_dp)
    mine = total = 2 * dp + frame
    step = 1
    while step < 2 * n_dp:
        zero, one = (masks[0][p] // step) % 2, (masks[1][p] // step) % 2
        if zero or one:
            flips = step if zero == one else step * (zero + frame * (one - zero))
            total = total + flips * (1 - 2 * ((mine // step) % 2))
        step *= 2
    return total


class Halving:
    def __init__(self, n_dp, refs, outs):
        self.n_dp, self.outs = n_dp, outs
        self.widths = [out.shape[1] for out in outs]
        self.units = len(outs)
        self.s, self.r0, self.k, self.r, self.kf, self.rf, self.fin = refs[:7]
        self.small, self.small_r, self.sems, self.small_sems, self.fin_sem = refs[7:]
        self.masks = stage_masks(n_dp)
        self.stages = len(self.masks)
        self.lags = [0, 2, 4] + [stage + 2 for stage in range(3, self.stages + 1)]
        self.dp, self.frame = lax.axis_index("dp"), lax.axis_index("frame")
        self.partners = [(self.dp, 1 - self.frame)] + [(self.flip(m), self.frame) for m in self.masks]
        self.started, self.waited, self.stored = [], set(), set()
        self.now, self.slot, self.made, self.core, self.ended = 0.0, 0, 0, 0, 0
        self.small_step = None

    def flip(self, mask):
        bit = mask[0] + self.frame * (mask[1] - mask[0])
        return self.dp + bit * (1 - 2 * ((self.dp // bit) % 2))

    def meet(self):
        barrier = pltpu.get_barrier_semaphore()
        for stage in range(self.stages + 1):
            pl.semaphore_signal(
                barrier, inc=1, device_id=self.partners[stage], device_id_type=pl.DeviceIdType.MESH
            )
        pl.semaphore_wait(barrier, self.stages + 1)

    def rows(self, stage):
        return self.s.shape[1] >> stage

    def wide(self, stage):
        return stage > 0 and self.rows(stage) < 16

    def remote(self, src, dst, sems, stage):
        return pltpu.make_async_remote_copy(
            src_ref=src, dst_ref=dst, send_sem=sems[0], recv_sem=sems[1],
            device_id=self.partners[stage], device_id_type=pl.DeviceIdType.MESH,
        )

    def copy(self, c, stage):
        h = self.rows(stage)
        half = pl.ds(h, h)
        if c is None:
            src, dst = self.small.at[stage], self.small_r.at[stage]
            sems = self.small_sems.at[0, stage], self.small_sems.at[1, stage]
        else:
            sems = self.sems.at[0, c, stage], self.sems.at[1, c, stage]
            lanes = pl.ds(0, self.widths[c])
            if stage == 0:
                src, dst = self.s.at[c % S_SLOTS, :, lanes], self.r0.at[c % C_SLOTS, :, lanes]
            elif self.wide(stage):
                src, dst = self.kf.at[c % K_SLOTS, half, lanes], self.rf.at[c % R_SLOTS, half, lanes]
            else:
                src, dst = self.k.at[c % K_SLOTS, half, lanes], self.r.at[c % R_SLOTS, half, lanes]
        return self.remote(src, dst, sems, stage)

    def send(self, c, stage):
        self.started.append((c, stage))
        self.copy(c, stage).start()

    def sent(self, c, stage):
        if (c, stage) not in self.waited:
            self.waited.add((c, stage))
            self.copy(c, stage).wait_send()

    def store(self, c):
        return pltpu.make_async_copy(
            self.fin.at[c % F_SLOTS, :, pl.ds(0, self.widths[c])], self.outs[c], self.fin_sem.at[c]
        )

    def free(self, c):
        while self.core < c - 2:
            self.join()
        if c >= S_SLOTS:
            self.sent(c - S_SLOTS, 0)
        if c >= K_SLOTS:
            while self.ended <= c - K_SLOTS:
                self.step()
            for stage in range(1, self.stages + 1):
                self.sent(c - K_SLOTS, stage)

    def join(self):
        c = self.core
        assert c < self.made
        self.copy(c, 0).wait_recv()
        slot, lanes = c % K_SLOTS, pl.ds(0, self.widths[c])
        own, got = self.k[slot, :, lanes], self.r0[c % C_SLOTS, :, lanes]
        self.k[slot, :, lanes] = (own.astype(F32) + got.astype(F32)).astype(BF)
        self.core += 1
        self.now += 0.4

    def fold(self, c, stage):
        h = self.rows(stage)
        near, half = pl.ds(0, h), pl.ds(h, h)
        slot, slot_r, lanes = c % K_SLOTS, c % R_SLOTS, pl.ds(0, self.widths[c])
        self.copy(c, stage).wait_recv()
        if self.wide(stage):
            total = self.kf[slot, near, lanes] + self.rf[slot_r, half, lanes]
        else:
            total = self.k[slot, near, lanes].astype(F32) + self.r[slot_r, half, lanes].astype(F32)
        if stage == self.stages:
            if c >= F_SLOTS:
                self.stored.add(c - F_SLOTS)
                self.store(c - F_SLOTS).wait()
            self.fin[c % F_SLOTS, :, lanes] = total
            self.store(c).start()
            self.ended = c + 1
            return
        if self.wide(stage + 1):
            self.kf[slot, near, lanes] = total
        else:
            self.k[slot, near, lanes] = total.astype(BF)
        self.send(c, stage + 1)

    def small_start(self):
        self.small_step = 0
        self.send(None, 0)

    def step(self):
        k = self.slot
        self.slot += 1
        if k < self.units:
            while self.core <= k:
                self.join()
            self.send(k, 1)
        for stage in range(1, self.stages + 1):
            c = k - self.lags[stage]
            if 0 <= c < self.units:
                self.fold(c, stage)
                self.now += 0.25
        self.small_fold()

    def small_fold(self):
        stage = self.small_step
        if stage is None or stage > self.stages:
            return
        self.copy(None, stage).wait_recv()
        self.small[stage + 1] = self.small[stage] + self.small_r[stage]
        self.small_step += 1
        if stage < self.stages:
            self.send(None, stage + 1)

    def spend(self, us):
        self.now += us
        while self.slot < self.made and START + PERIOD * sum(self.widths[: self.slot]) / D <= self.now:
            self.step()

    def finish(self):
        while self.ended < self.units:
            self.step()
        while self.small_step <= self.stages:
            self.small_fold()
        for c, stage in self.started:
            self.sent(c, stage)
        for c in range(self.units):
            if c not in self.stored:
                self.store(c).wait()


def halving_scratch(n_dp, d, units):
    n = 2 * n_dp
    m = d // 2
    stages = n_dp.bit_length() - 1
    sem = pltpu.SemaphoreType.DMA
    wide = (m >> stages) < 16
    return [
        pltpu.VMEM((S_SLOTS, m, d), BF),
        pltpu.VMEM((C_SLOTS, m, d), BF),
        pltpu.VMEM((K_SLOTS, m, d), BF),
        pltpu.VMEM((R_SLOTS, m, d), BF),
        pltpu.VMEM((K_SLOTS, 16, d) if wide else (1, 8, 128), F32),
        pltpu.VMEM((R_SLOTS, 16, d) if wide else (1, 8, 128), F32),
        pltpu.VMEM((F_SLOTS, d // n, d), F32),
        pltpu.VMEM((stages + 2, 24, d), F32),
        pltpu.VMEM((stages + 1, 24, d), F32),
        sem((2, units, stages + 1)),
        sem((2, stages + 1)),
        sem((units,)),
    ]


class Pool:
    def __init__(self, sems):
        self.sems, self.used = sems, 0

    def start(self, src, dst):
        copy = pltpu.make_async_copy(src, dst, self.sems.at[self.used])
        self.used += 1
        copy.start()
        return copy


def turn(halving, r, src, at, perm):
    at[...] = src[...].T.astype(at.dtype)
    gather(halving, r, 0, 1, at, perm)


def gather(halving, r, u, count, at, perm):
    for p in range(2 * halving.n_dp):
        base = shard_at(halving.n_dp, halving.dp, halving.frame, p) * (r * count)
        perm[pl.ds(p * r, r), :] = at[pl.ds(pl.multiple_of(base + u * r, 8), r), :].astype(perm.dtype)
    halving.spend(0.5)


def grad(halving, left, *rights):
    c = halving.made
    m = left.shape[0] // 2
    halving.free(c)
    wide = rights[0].shape[1]
    assert wide * len(rights) == halving.widths[c]
    for far in (True, False):
        rows = left[pl.ds(m, m), :] if far else left[pl.ds(0, m), :]
        for i, right in enumerate(rights):
            lanes = pl.ds(i * wide, wide)
            part = dot(rows, right[...]).astype(BF)
            if far:
                halving.s[c % S_SLOTS, :, lanes] = part
            else:
                halving.k[c % K_SLOTS, :, lanes] = part
        if far:
            halving.send(c, 0)
    halving.made += 1
    halving.spend(1.4 * halving.widths[c] / D)


SMALL_ROWS = 24
LAST = [(0, D // 2), (D // 2, D // 4), (D * 3 // 4, D // 4)]
UNITS = 15 + len(LAST)


def back_kernel(n_dp, nb, steps, *refs):
    (
        gain, sums3, g, df_h, u_h, a2, dh3_h, h2_h, we, wr, w_in, w_out,
        ce, cr, cq, ck, cv, cc, a1, h1_h, mem, se, sr, sq, sk, sv, sc, a0, tok_h,
    ) = refs[:29]
    red_o, exp_o, in_o, out_o, small_o, gt_o, gm_o = refs[29:36]
    df, dh, dx, dc, raw, at, perm, lsem, osem, gsem = refs[48:]
    t, d = df.shape
    ff = g.shape[1]
    r = d // (2 * n_dp)
    tile = ff // steps
    rows = t // nb
    cols = mem.shape[0] // nb
    outs = [red_o.at[pl.ds(u * r, r)] for u in range(4)]
    outs += [exp_o.at[:, pl.ds(u * d, d)] for u in range(4)]
    outs += [out_o.at[1], in_o.at[1, 0], in_o.at[1, 1], in_o.at[1, 2]]
    outs += [out_o.at[0], in_o.at[0, 0], in_o.at[0, 1]]
    outs += [in_o.at[0, 2, :, pl.ds(at, width)] for at, width in LAST]
    halving = Halving(n_dp, refs[36:48], outs)
    small = halving.small
    pool = Pool(lsem)
    spend = halving.spend
    act, macts = (t, d), (nb * cols, d)

    def reduce_phase(gbuf, gat, gperm):
        loads = [pool.start(g, gbuf), pool.start(df_h, df)]
        halving.meet()
        for x in loads:
            x.wait()
        gat[...] = gbuf[...].T.astype(gat.dtype)
        spend(1.0)
        for u in range(4):
            gather(halving, r, u, 4, gat, gperm)
            grad(halving, gperm, df)

    small[0] = jnp.zeros((SMALL_ROWS, d), F32)
    small[0, 9:10, :] = sums3[0:1, :]
    small[0, 13:14, :] = sums3[1:2, :]
    small[0, 18:19, :] = sums3[2:3, :]
    pl.run_scoped(
        reduce_phase, pltpu.VMEM((t, ff), BF), pltpu.VMEM((ff, t), at.dtype), pltpu.VMEM((d, t), BF)
    )

    def feed_phase(ubuf, wrbuf, webuf, du, dh3, h2, wbuf):
        def fetch(j):
            return [
                pool.start(wr.at[pl.ds(j * tile, tile)], wrbuf.at[j % 3]),
                pool.start(u_h.at[j], ubuf.at[j % 3]),
                pool.start(we.at[:, pl.ds(j * tile, tile)], webuf.at[j % 3]),
            ]

        flight = fetch(0)
        turned = pool.start(a2, raw)
        later = [pool.start(h2_h, h2), pool.start(dh3_h, dh3), pool.start(w_out.at[1], wbuf)]
        each = d // tile
        for j in range(steps + 1):
            if j < steps:
                for x in flight:
                    x.wait()
            if j + 1 < steps:
                flight = fetch(j + 1)
            if j < steps:
                x = ubuf[j % 3].astype(F32)
                x2 = x * x
                th = jnp.tanh(x * (GELU_C + GELU_D * x2))
                slope = (0.5 + 0.5 * th) * (1.0 + (1.0 - th) * (x * (GELU_C + (3 * GELU_D) * x2)))
                y = dot_t(df[...], wrbuf[j % 3]) * slope
                du[j] = y.astype(BF)
                row, lane = divmod(j * tile, d)
                small[0, 14 + row : 15 + row, lane : lane + tile] = row_sum(y)
            if j == 1:
                dh[...] = dot_t(du[0], webuf[0])
            elif j > 1:
                dh[...] += dot_t(du[j - 1], webuf[(j - 1) % 3])
            spend(2.0)
            if j == 0:
                turned.wait()
                turn(halving, r, raw, at, perm)
            if j > 0 and j % each == 0:
                grad(halving, perm, *[du.at[j - each + i] for i in range(each)])
        later[0].wait()
        later[1].wait()
        turned = pool.start(cc, raw)
        back, small[0, 8:9, :], small[0, 12:13, :] = norm_back(dh[...], h2[...], gain[2:3, :])
        dh[...] = dh3[...] + back
        dx[...] = dh[...].astype(BF)
        small[0, 5:6, :] = row_sum(dx[...])
        spend(1.2)
        later[2].wait()
        dc[...] = dot_t(dx[...], wbuf[...]).astype(BF)
        spend(1.3)
        turned.wait()
        turn(halving, r, raw, at, perm)
        grad(halving, perm, dx)

    pl.run_scoped(
        feed_phase,
        pltpu.VMEM((3, t, tile), BF),
        pltpu.VMEM((3, tile, d), BF),
        pltpu.VMEM((3, d, tile), BF),
        pltpu.VMEM((steps, t, tile), BF),
        pltpu.VMEM(act, F32),
        pltpu.VMEM(act, F32),
        pltpu.VMEM((d, d), BF),
    )

    def cross_phase(e, r_, q, k, v, c, dq, dk, dv, wbuf, gm):
        loads = Group(pool)
        start_parts(loads, nb, ce, e, (cr, r_), (cc, c), (cv, v), (ck, k), (cq, q))
        turned = pool.start(a1, raw)
        later = [pool.start(w_in.at[1, 0], wbuf.at[0]), pool.start(h1_h, gm), pool.start(w_out.at[0], wbuf.at[1])]
        later.append(pool.start(w_in.at[1, 1], wbuf.at[2]))
        for i in range(PARTS):
            loads.wait(6)
            attend_back(nb, rows, cols, i, e, r_, q, k, v, c, dc, dq, dk, dv)
            spend(2.2)
        turned.wait()
        turn(halving, r, raw, at, perm)
        turned = pool.start(mem, raw)
        grad(halving, perm, dq)
        later[0].wait()
        later[1].wait()
        up = dot_t(dq[...], wbuf[0])
        back, small[0, 7:8, :], small[0, 11:12, :] = norm_back(up, gm[...], gain[1:2, :])
        later.append(pool.start(w_in.at[1, 2], wbuf.at[0]))
        dh[...] += back
        dx[...] = dh[...].astype(BF)
        small[0, 2:3, :] = row_sum(dx[...])
        small[0, 3:4, :] = row_sum(dq[...])
        small[0, 4:5, :] = row_sum(dv[...])
        spend(2.6)
        turned.wait()
        turn(halving, r, raw, at, perm)
        turned = pool.start(sc, raw)
        grad(halving, perm, dk)
        grad(halving, perm, dv)
        later[3].wait()
        gm[...] = dot_t(dk[...], wbuf[2])
        later[4].wait()
        gm[...] += dot_t(dv[...], wbuf[0])
        spend(2.6)
        half = cols // 2
        moves = []
        for b in range(nb):
            moves.append(pool.start(gm.at[pl.ds(b * cols, half)], gm_o.at[b, 0, halving.frame]))
            far = halving.remote(
                gm.at[pl.ds(b * cols + half, half)], gm_o.at[b, 0, halving.frame], (gsem.at[0, b], gsem.at[1, b]), 0
            )
            far.start()
            moves.append(far)
        later[2].wait()
        dc[...] = dot_t(dx[...], wbuf[1]).astype(BF)
        spend(1.3)
        turned.wait()
        turn(halving, r, raw, at, perm)
        grad(halving, perm, dx)
        for x in moves:
            x.wait()

    pl.run_scoped(
        cross_phase,
        pltpu.VMEM(ce.shape, BF),
        pltpu.VMEM(act, F32),
        pltpu.VMEM(act, BF),
        pltpu.VMEM(macts, BF),
        pltpu.VMEM(macts, BF),
        pltpu.VMEM(act, BF),
        pltpu.VMEM(act, BF),
        pltpu.VMEM(macts, BF),
        pltpu.VMEM(macts, BF),
        pltpu.VMEM((3, d, d), BF),
        pltpu.VMEM(macts, F32),
    )

    def self_phase(e, r_, q, k, v, c, dq, dk, dv, tok, wbuf):
        loads = Group(pool)
        start_parts(loads, nb, se, e, (sr, r_), (sc, c), (sv, v), (sk, k), (sq, q))
        turned = pool.start(a0, raw)
        later = [pool.start(w_in.at[0, i], wbuf.at[i]) for i in range(3)] + [pool.start(tok_h, tok)]
        for i in range(PARTS):
            loads.wait(6)
            attend_back(nb, rows, rows, i, e, r_, q, k, v, c, dc, dq, dk, dv)
            spend(2.2)
        turned.wait()
        turn(halving, r, raw, at, perm)
        grad(halving, perm, dq)
        grad(halving, perm, dk)
        for first, width in LAST:
            grad(halving, perm, dv.at[:, pl.ds(first, width)])
        for x in later:
            x.wait()
        up = dot_t(dq[...], wbuf[0]) + dot_t(dk[...], wbuf[1]) + dot_t(dv[...], wbuf[2])
        back, small[0, 6:7, :], small[0, 10:11, :] = norm_back(up, tok[...].astype(F32), gain[0:1, :])
        dh[...] += back
        moved = pool.start(dh, gt_o)
        small[0, 0:1, :] = row_sum(dq[...])
        small[0, 1:2, :] = row_sum(dv[...])
        halving.small_start()
        spend(5.2)
        moved.wait()

    pl.run_scoped(
        self_phase,
        pltpu.VMEM(se.shape, BF),
        pltpu.VMEM(act, F32),
        *[pltpu.VMEM(act, BF)] * 8,
        pltpu.VMEM((3, d, d), BF),
    )
    halving.finish()
    out = pltpu.make_async_copy(small.at[halving.stages + 1], small_o, osem)
    out.start()
    out.wait()


class Group:
    def __init__(self, pool):
        self.pool, self.copies, self.done = pool, [], 0

    def start(self, *pairs):
        for src, dst in pairs:
            self.copies.append(self.pool.start(src, dst))

    def wait(self, count):
        for copy in self.copies[self.done : self.done + count]:
            copy.wait()
        self.done += count


def backward(n_dp, nb, memory_shape, *args, tile=512):
    df, g, w_in = args[3], args[2], args[10]
    t, d = df.shape
    ff = g.shape[1]
    n = 2 * n_dp
    r = d // n
    kind = BF if r % 16 == 0 else F32
    act = (t, d)
    sem = pltpu.SemaphoreType.DMA
    return pl.pallas_call(
        functools.partial(back_kernel, n_dp, nb, ff // tile),
        out_shape=[
            hbm((4 * r, d), F32), hbm((r, ff), F32), hbm((2, 3, r, d), F32), hbm((2, r, d), F32),
            hbm((SMALL_ROWS, d), F32), hbm(act, F32), hbm(memory_shape, F32),
        ],
        in_specs=[VM] * 2 + [ANY] * (len(args) - 2),
        out_specs=[ANY] * 7,
        scratch_shapes=halving_scratch(n_dp, d, UNITS)
        + [
            pltpu.VMEM(act, BF),
            pltpu.VMEM(act, F32),
            pltpu.VMEM(act, BF),
            pltpu.VMEM(act, BF),
            pltpu.VMEM(act, BF),
            pltpu.VMEM((d, t), kind),
            pltpu.VMEM((d, t), BF),
            sem((128,)),
            sem,
            sem((2, nb)),
        ],
        compiler_params=pltpu.CompilerParams(vmem_limit_bytes=63 * 2**20, collective_id=0, has_side_effects=True),
        name="backward",
    )(*args)


def finish_kernel(n, count, small, *refs):
    ins, outs = refs[:count], refs[count : 2 * count]
    bias, gain, shift, eb, rb = refs[2 * count : 2 * count + 5]
    bufs = refs[2 * count + 5 : -2]
    loads, stores = Copies(refs[-2]), Copies(refs[-1])
    loads.start(*zip(ins, bufs))
    me = 2 * lax.axis_index("dp") + lax.axis_index("frame")
    d = small.shape[1]
    w, wide = bias.shape[2], eb.shape[1]

    def window(rows, first, width):
        return pltpu.roll(rows, d - first, 1)[:, :width]

    mine = window(small[...], me * w, w)
    bias[0], bias[1] = mine[0:3], mine[3:6]
    gain[...], shift[...] = mine[6:10], mine[10:14]
    rb[...] = mine[18:19]
    place = me * wide
    row = small[14:15, :]
    for i in range(1, n * wide // d):
        row = jnp.where(place // d == i, small[14 + i : 15 + i, :], row)
    eb[...] = window(row, place % d, wide)
    for buf, out in zip(bufs, outs):
        loads.wait()
        stores.start((buf, out))
    stores.wait_all()


def finish(n, ff, small, *arrays):
    d = small.shape[1]
    w = d // n
    count = len(arrays)
    return pl.pallas_call(
        functools.partial(finish_kernel, n, count),
        out_shape=[hbm(x.shape, x.dtype) for x in arrays]
        + [hbm((2, 3, w), F32), hbm((4, w), F32), hbm((4, w), F32), hbm((1, ff // n), F32), hbm((1, w), F32)],
        in_specs=[VM] + [ANY] * count,
        out_specs=[ANY] * count + [VM] * 5,
        scratch_shapes=[pltpu.VMEM(x.shape, x.dtype) for x in arrays] + [pltpu.SemaphoreType.DMA((count,))] * 2,
        compiler_params=params(),
        name="finish",
    )(small, *arrays)


def local(
    n_dp,
    tokens,
    memory,
    token_lengths,
    frame_lengths,
    attention_in,
    attention_out,
    attention_bias,
    norm_gain,
    norm_bias,
    expand_weight,
    expand_bias,
    reduce_weight,
    reduce_bias,
    cotangent,
):
    n = 2 * n_dp
    nb = tokens.shape[0]
    t = nb * tokens.shape[3]
    ff = expand_weight.shape[1]
    w_in, w_out, bias = attention_in, attention_out, attention_bias.reshape(6, D)
    tok = tokens.reshape(t, D)

    far_mem = permute(memory, core_pairs(n_dp))
    q, k, v, e, r, c, h1, a0, a1, cq = self_forward(
        nb, token_lengths, bias, norm_gain, norm_bias, tok, w_in, w_out
    )
    mem, ck, cv, ce, cr, cc, h2, a2, u, g, out, dh3, df, sums3 = rest_forward(
        nb, token_lengths, frame_lengths, bias, norm_gain, norm_bias,
        reduce_bias.reshape(1, D), expand_bias.reshape(1, ff),
        memory, far_mem, cq, h1, cotangent.reshape(t, D), w_in, w_out, expand_weight, reduce_weight,
    )
    grad_reduce, grad_expand, grad_in, grad_out, small, grad_tokens, grad_memory = backward(
        n_dp, nb, memory.shape, norm_gain, sums3, g, df, u, a2, dh3, h2, expand_weight, reduce_weight, w_in, w_out,
        ce, cr, cq, ck, cv, cc, a1, h1, mem, e, r, q, k, v, c, a0, tok,
    )
    grad_reduce, grad_expand, grad_in, grad_out, grad_tokens, grad_memory, *rest = finish(
        n, ff, small, grad_reduce, grad_expand, grad_in, grad_out, grad_tokens, grad_memory
    )
    grad_bias, grad_gain, grad_shift, grad_eb, grad_rb = rest
    shape = tokens.shape
    return (
        out.reshape(shape),
        grad_tokens.reshape(shape),
        grad_memory,
        grad_in,
        grad_out,
        grad_bias,
        grad_gain,
        grad_shift,
        grad_expand,
        grad_eb.reshape(-1),
        grad_reduce,
        grad_rb.reshape(-1),
    )


def solution(mesh):
    spread = P(None, "dp", "frame", None, None)
    by_frame = P(None, "dp", None, "frame", None)
    both = ("dp", "frame")
    lengths = P(None, "dp", None, None)
    return jax.shard_map(
        functools.partial(local, mesh.shape["dp"]),
        mesh=mesh,
        in_specs=(spread, by_frame, lengths, lengths) + (P(),) * 9 + (spread,),
        out_specs=(
            spread,
            spread,
            by_frame,
            P(None, None, both, None),
            P(None, both, None),
            P(None, None, both),
            P(None, both),
            P(None, both),
            P(both, None),
            P(both),
            P(both, None),
            P(both),
        ),
        check_vma=False,
    )
```

```python
import functools
import math

import jax
import jax.numpy as jnp
from jax import lax
from jax.experimental import pallas as pl
from jax.experimental.pallas import tpu as pltpu
from jax.sharding import PartitionSpec as P

D = 1024
HEADS = 16
HEAD_DIM = 64
FACTOR = 1.0 / math.sqrt(HEAD_DIM)
BF = jnp.bfloat16
F32 = jnp.float32


def dot(a, b):
    return jnp.dot(a, b, preferred_element_type=F32)


def dot_t(a, b):
    return lax.dot_general(a, b, (((1,), (1,)), ((), ())), preferred_element_type=F32)


VM = pl.BlockSpec(memory_space=pltpu.VMEM)
SM = pl.BlockSpec(memory_space=pltpu.SMEM)
ANY = pl.BlockSpec(memory_space=pl.ANY)
GELU_C = 0.7978845608028654
GELU_D = 0.044715 * GELU_C


def params(mib=58):
    return pltpu.CompilerParams(vmem_limit_bytes=mib * 2**20)


def hbm(shape, kind):
    return jax.ShapeDtypeStruct(shape, kind)


class Copies:
    def __init__(self, sems):
        self.sems, self.copies, self.done = sems, [], 0

    def start(self, *pairs):
        for src, dst in pairs:
            copy = pltpu.make_async_copy(src, dst, self.sems.at[len(self.copies)])
            copy.start()
            self.copies.append(copy)

    def wait(self, count=1):
        for copy in self.copies[self.done : self.done + count]:
            copy.wait()
        self.done += count

    def wait_all(self):
        self.wait(len(self.copies) - self.done)


def stats(v):
    off = v - jnp.mean(v, axis=-1, keepdims=True)
    r = lax.rsqrt(jnp.mean(off * off, axis=-1, keepdims=True) + 1e-5)
    return off * r, r


def norm_back(e, v, gain):
    n, r = stats(v)
    eg = e * gain
    back = r * (
        eg - jnp.mean(eg, axis=-1, keepdims=True) - n * jnp.mean(eg * n, axis=-1, keepdims=True)
    )
    return back, row_sum(e * n), row_sum(e)


def row_sum(x):
    return jnp.sum(x.astype(F32), axis=0, keepdims=True)


def pair_mask(rows):
    return lax.broadcasted_iota(jnp.int32, (rows, 128), 1) < HEAD_DIM


def segments(lengths, b, a, shape, dim, shift=0):
    pos = lax.broadcasted_iota(jnp.int32, shape, dim) + shift
    pos = jnp.where(pos >= shape[dim], pos - shape[dim], pos)
    total, seg = 0, jnp.zeros(shape, jnp.int32)
    for i in range(lengths.shape[3] - 1):
        total = total + lengths[b, 0, a, i]
        seg = seg + (pos >= total).astype(jnp.int32)
    return seg


def attend(nb, rows, cols, q, k, v, e_ref, r_ref, c, mask, unroll=4):
    low = pair_mask(rows)
    one = jnp.ones((cols, 128), BF)

    def pair(j, _):
        lanes = pl.ds(pl.multiple_of(j * 128, 128), 128)
        for b in range(nb):
            qs, ks = pl.ds(b * rows, rows), pl.ds(b * cols, cols)
            q2, k2, v2 = q[qs, lanes], k[ks, lanes], v[ks, lanes]
            zero = jnp.zeros_like(q2)
            both = jnp.concatenate([jnp.where(low, q2, zero), jnp.where(low, zero, q2)], axis=0)
            s = dot_t(both, k2).reshape(2, rows, cols) + mask[b][None]
            e = jnp.exp(s - jnp.max(s, axis=-1, keepdims=True)).astype(BF)
            e_ref[b, pl.ds(2 * j, 2)] = e
            o = dot(e.reshape(2 * rows, cols), jnp.concatenate([v2, one], axis=1))
            r = 1.0 / jnp.where(low, o[:rows, 128:], o[rows:, 128:])
            r_ref[qs, lanes] = r
            c[qs, lanes] = (jnp.where(low, o[:rows, :128], o[rows:, :128]) * r).astype(BF)
        return 0

    lax.fori_loop(0, HEADS // 2, pair, 0, unroll=unroll)


def attend_back(nb, rows, cols, part, e_ref, r_ref, q, k, v, c, dc, dq, dk, dv):
    low, low_k = pair_mask(rows), pair_mask(cols)
    minus = jnp.full((cols, 128), -1, BF)

    count = HEADS // 2 // PARTS
    for j in range(part * count, (part + 1) * count):
        lanes = pl.ds(j * 128, 128)
        for b in range(nb):
            qs, ks = pl.ds(b * rows, rows), pl.ds(b * cols, cols)
            q2, k2, v2 = q[qs, lanes], k[ks, lanes], v[ks, lanes]
            dcs = dc[qs, lanes].astype(F32) * r_ref[qs, lanes]
            delta = (dcs * c[qs, lanes].astype(F32)).astype(BF)
            dcs = dcs.astype(BF)
            zero = jnp.zeros_like(dcs)
            first = jnp.concatenate([jnp.where(low, dcs, zero), jnp.where(low, delta, zero)], axis=1)
            second = jnp.concatenate([jnp.where(low, zero, dcs), jnp.where(low, zero, delta)], axis=1)
            slope = dot_t(
                jnp.concatenate([first, second], axis=0), jnp.concatenate([v2, minus], axis=1)
            )
            e = e_ref[b, pl.ds(2 * j, 2)]
            ds = (e.astype(F32) * slope.reshape(2, rows, cols)).astype(BF)
            g = dot(ds.reshape(2 * rows, cols), k2)
            dq[qs, lanes] = (jnp.where(low, g[:rows], g[rows:]) * FACTOR).astype(BF)
            g = dot(jnp.concatenate([ds[0].T, ds[1].T], axis=0), q2)
            dk[ks, lanes] = jnp.where(low_k, g[:cols], g[cols:]).astype(BF)
            g = dot(jnp.concatenate([e[0].T, e[1].T], axis=0), dcs)
            dv[ks, lanes] = jnp.where(low_k, g[:cols], g[cols:]).astype(BF)


PARTS = 4


def start_parts(loads, nb, e_h, e, *pairs):
    for i in range(PARTS):
        heads = pl.ds(i * HEADS // PARTS, HEADS // PARTS)
        loads.start((e_h.at[:, heads], e.at[:, heads]))
        for src, dst in pairs:
            lanes = pl.ds(i * (D // PARTS), D // PARTS)
            loads.start((src.at[:, lanes], dst.at[:, lanes]))


K_SLOTS = 9
R_SLOTS = 6
S_SLOTS = 4
C_SLOTS = 4
F_SLOTS = 4
PERIOD = 6.6
START = 2.0


ORDERS = {
    "xz": ([0, 2, 1, 3], [1, 2, 0, 3]),
    "zx": ([2, 0, 1, 3], [2, 1, 0, 3]),
    "xy": ([0, 1, 2, 3], [1, 0, 2, 3]),
}


def stage_masks(n_dp, order):
    m = n_dp.bit_length() - 1
    if m == 4:
        orders = ORDERS[order]
    else:
        one = list(range(0, m, 2)) + list(range(1, m, 2))
        orders = one, one[1:] + one[:1]
    return [(1 << a, 1 << b) for a, b in zip(*orders)]


def place_masks(n_dp, order):
    masks = stage_masks(n_dp, order)
    m = len(masks)
    out = []
    for f in range(2):
        row = []
        for p in range(2 * n_dp):
            far = p >> m
            mask = far
            for s in range(m):
                if (p >> (m - 1 - s)) & 1:
                    mask ^= 2 * masks[s][1 - f if far else f]
            row.append(mask)
        out.append(row)
    return out


def shard_at(n_dp, order, dp, frame, p):
    masks = place_masks(n_dp, order)
    mine = total = 2 * dp + frame
    step = 1
    while step < 2 * n_dp:
        zero, one = (masks[0][p] // step) % 2, (masks[1][p] // step) % 2
        if zero or one:
            flips = step if zero == one else step * (zero + frame * (one - zero))
            total = total + flips * (1 - 2 * ((mine // step) % 2))
        step *= 2
    return total


class Halving:
    def __init__(self, n_dp, refs, outs, orders):
        self.n_dp, self.outs = n_dp, outs
        self.widths = [out.shape[1] for out in outs]
        self.units = len(outs)
        self.s, self.r0, self.k, self.r, self.kf, self.rf, self.fin = refs[:7]
        self.small, self.small_r, self.sems, self.small_sems, self.fin_sem = refs[7:]
        self.orders = orders
        self.stages = n_dp.bit_length() - 1
        self.lags = [0, 2, 4] + [stage + 2 for stage in range(3, self.stages + 1)]
        self.dp, self.frame = lax.axis_index("dp"), lax.axis_index("frame")
        self.partners = {
            order: [(self.dp, 1 - self.frame)] + [(self.flip(m), self.frame) for m in stage_masks(n_dp, order)]
            for order in ORDERS
        }
        self.started, self.waited, self.stored = [], set(), set()
        self.now, self.slot, self.made, self.core, self.ended = 0.0, 0, 0, 0, 0
        self.small_step = None

    def flip(self, mask):
        bit = mask[0] + self.frame * (mask[1] - mask[0])
        return self.dp + bit * (1 - 2 * ((self.dp // bit) % 2))

    def greet(self):
        barrier = pltpu.get_barrier_semaphore()
        for stage in range(self.stages + 1):
            pl.semaphore_signal(
                barrier, inc=1, device_id=self.partners["xz"][stage], device_id_type=pl.DeviceIdType.MESH
            )

    def meet(self):
        pl.semaphore_wait(pltpu.get_barrier_semaphore(), self.stages + 1)

    def rows(self, stage):
        return self.s.shape[1] >> stage

    def wide(self, stage):
        return stage > 0 and self.rows(stage) < 16

    def remote(self, src, dst, sems, partner):
        return pltpu.make_async_remote_copy(
            src_ref=src, dst_ref=dst, send_sem=sems[0], recv_sem=sems[1],
            device_id=partner, device_id_type=pl.DeviceIdType.MESH,
        )

    def copy(self, c, stage):
        h = self.rows(stage)
        half = pl.ds(h, h)
        if c is None:
            src, dst = self.small.at[stage], self.small_r.at[stage]
            sems = self.small_sems.at[0, stage], self.small_sems.at[1, stage]
        else:
            sems = self.sems.at[0, c, stage], self.sems.at[1, c, stage]
            lanes = pl.ds(0, self.widths[c])
            if stage == 0:
                src, dst = self.s.at[c % S_SLOTS, :, lanes], self.r0.at[c % C_SLOTS, :, lanes]
            elif self.wide(stage):
                src, dst = self.kf.at[c % K_SLOTS, half, lanes], self.rf.at[c % R_SLOTS, half, lanes]
            else:
                src, dst = self.k.at[c % K_SLOTS, half, lanes], self.r.at[c % R_SLOTS, half, lanes]
        return self.remote(src, dst, sems, self.partners["xz" if c is None else self.orders[c]][stage])

    def send(self, c, stage):
        self.started.append((c, stage))
        self.copy(c, stage).start()

    def sent(self, c, stage):
        if (c, stage) not in self.waited:
            self.waited.add((c, stage))
            self.copy(c, stage).wait_send()

    def store(self, c):
        return pltpu.make_async_copy(
            self.fin.at[c % F_SLOTS, :, pl.ds(0, self.widths[c])], self.outs[c], self.fin_sem.at[c]
        )

    def free(self, c):
        while self.core < c - 1:
            self.join()
        if c >= S_SLOTS:
            self.sent(c - S_SLOTS, 0)
        if c >= K_SLOTS:
            while self.ended <= c - K_SLOTS:
                self.step()
            for stage in range(1, self.stages + 1):
                self.sent(c - K_SLOTS, stage)

    def join(self):
        c = self.core
        assert c < self.made
        self.copy(c, 0).wait_recv()
        slot, lanes = c % K_SLOTS, pl.ds(0, self.widths[c])
        own, got = self.k[slot, :, lanes], self.r0[c % C_SLOTS, :, lanes]
        self.k[slot, :, lanes] = (own.astype(F32) + got.astype(F32)).astype(BF)
        self.core += 1
        self.now += 0.4

    def fold(self, c, stage):
        h = self.rows(stage)
        near, half = pl.ds(0, h), pl.ds(h, h)
        slot, slot_r, lanes = c % K_SLOTS, c % R_SLOTS, pl.ds(0, self.widths[c])
        self.copy(c, stage).wait_recv()
        if self.wide(stage):
            total = self.kf[slot, near, lanes] + self.rf[slot_r, half, lanes]
        else:
            total = self.k[slot, near, lanes].astype(F32) + self.r[slot_r, half, lanes].astype(F32)
        if stage == self.stages:
            if c >= F_SLOTS:
                self.stored.add(c - F_SLOTS)
                self.store(c - F_SLOTS).wait()
            self.fin[c % F_SLOTS, :, lanes] = total
            self.store(c).start()
            self.ended = c + 1
            return
        if self.wide(stage + 1):
            self.kf[slot, near, lanes] = total
        else:
            self.k[slot, near, lanes] = total.astype(BF)
        self.send(c, stage + 1)

    def small_start(self):
        self.small_step = 0
        self.send(None, 0)

    def step(self):
        k = self.slot
        self.slot += 1
        if k < self.units:
            while self.core <= k:
                self.join()
            self.send(k, 1)
        for stage in range(1, self.stages + 1):
            c = k - self.lags[stage]
            if 0 <= c < self.units:
                self.fold(c, stage)
                self.now += 0.25
        self.small_fold()

    def small_fold(self):
        stage = self.small_step
        if stage is None or stage > self.stages:
            return
        self.copy(None, stage).wait_recv()
        self.small[stage + 1] = self.small[stage] + self.small_r[stage]
        self.small_step += 1
        if stage < self.stages:
            self.send(None, stage + 1)

    def spend(self, us):
        self.now += us
        while self.slot < self.made and START + PERIOD * sum(self.widths[: self.slot]) / D <= self.now:
            self.step()

    def finish(self):
        while self.ended < self.units:
            self.step()
        while self.small_step <= self.stages:
            self.small_fold()
        for c, stage in self.started:
            self.sent(c, stage)
        for c in range(self.units):
            if c not in self.stored:
                self.store(c).wait()


def halving_scratch(n_dp, d, units):
    n = 2 * n_dp
    m = d // 2
    stages = n_dp.bit_length() - 1
    sem = pltpu.SemaphoreType.DMA
    wide = (m >> stages) < 16
    return [
        pltpu.VMEM((S_SLOTS, m, d), BF),
        pltpu.VMEM((C_SLOTS, m, d), BF),
        pltpu.VMEM((K_SLOTS, m, d), BF),
        pltpu.VMEM((R_SLOTS, m, d), BF),
        pltpu.VMEM((K_SLOTS, 16, d) if wide else (1, 8, 128), F32),
        pltpu.VMEM((R_SLOTS, 16, d) if wide else (1, 8, 128), F32),
        pltpu.VMEM((F_SLOTS, d // n, d), F32),
        pltpu.VMEM((stages + 2, 24, d), F32),
        pltpu.VMEM((stages + 1, 24, d), F32),
        sem((2, units, stages + 1)),
        sem((2, stages + 1)),
        sem((units,)),
    ]


class Pool:
    def __init__(self, sems):
        self.sems, self.used = sems, 0

    def start(self, src, dst):
        copy = pltpu.make_async_copy(src, dst, self.sems.at[self.used])
        self.used += 1
        copy.start()
        return copy


class Group:
    def __init__(self, pool):
        self.pool, self.copies, self.done = pool, [], 0

    def start(self, *pairs):
        for src, dst in pairs:
            self.copies.append(self.pool.start(src, dst))

    def wait(self, count):
        for copy in self.copies[self.done : self.done + count]:
            copy.wait()
        self.done += count

    def wait_all(self):
        self.wait(len(self.copies) - self.done)


class Stream:
    def __init__(self, blocks, buf, sems):
        self.blocks, self.buf, self.sems = blocks, buf, sems
        self.depth, self.taken = buf.shape[0], 0
        for i in range(self.depth - 1):
            self.copy(i).start()

    def copy(self, i):
        return pltpu.make_async_copy(self.blocks[i](), self.buf.at[i % self.depth], self.sems.at[i])

    def take(self):
        i = self.taken
        self.taken += 1
        ahead = i + self.depth - 2
        if i > 0 and ahead < len(self.blocks):
            if ahead >= self.depth - 1:
                self.copy(ahead).start()
        self.copy(i).wait()
        return self.buf.at[i % self.depth]


def turn(halving, r, src, at, perm):
    at[...] = src[...].T.astype(at.dtype)
    gather(halving, r, 0, 1, at, perm)


def gather(halving, r, u, count, at, perm):
    order = halving.orders[halving.made]
    for p in range(2 * halving.n_dp):
        base = shard_at(halving.n_dp, order, halving.dp, halving.frame, p) * (r * count)
        perm[pl.ds(p * r, r), :] = at[pl.ds(pl.multiple_of(base + u * r, 8), r), :].astype(perm.dtype)
    halving.spend(0.5)


def grad(halving, left, right):
    c = halving.made
    m = left.shape[0] // 2
    wide = right.shape[1]
    lanes = pl.ds(0, wide)
    assert wide == halving.widths[c]
    halving.free(c)
    halving.s[c % S_SLOTS, :, lanes] = dot(left[pl.ds(m, m), :], right[...]).astype(BF)
    halving.send(c, 0)
    halving.k[c % K_SLOTS, :, lanes] = dot(left[pl.ds(0, m), :], right[...]).astype(BF)
    halving.made += 1
    halving.spend(1.4 * wide / D)


SMALL_ROWS = 24
UNITS = 16
HELD = 18


def layer_kernel(n_dp, nb, *refs):
    (
        tok_len, frm_len, bias, gain, shift, rb, eb,
        tok_h, memory, cot_h, w_in, w_out, we, wr,
    ) = refs[:14]
    out_o, red_o, exp_o, in_o, out_w, small_o, gt_o, gm_o = refs[14:22]
    (
        far_mem, h1_h, h2_h, sr, cr, se, ce, u_h, sq, sk, sv, sc, a0_h, a1_h, cq_h, ck_h, cv_h, cc_h,
    ) = refs[22 : 22 + HELD]
    a2_h = refs[22 + HELD]
    rest = refs[23 + HELD :]
    hrefs = rest[:12]
    wbuf, df, dh, dx, dc, raw, at, perm, wsem, lsem, xsem, osem = rest[12:]
    t, d = df.shape
    steps = we.shape[1] // d
    r = d // (2 * n_dp)
    rows = t // nb
    half = memory.shape[3]
    cols = 2 * half
    act, macts = (t, d), (nb * cols, d)
    outs = [red_o.at[pl.ds(u * r, r)] for u in range(4)]
    outs += [exp_o.at[:, pl.ds(u * d, d)] for u in range(4)]
    outs += [out_w.at[1], in_o.at[1, 0], in_o.at[1, 1], in_o.at[1, 2]]
    outs += [out_w.at[0], in_o.at[0, 0], in_o.at[0, 1], in_o.at[0, 2]]
    halving = Halving(n_dp, hrefs, outs, ["xz"] * (UNITS - 2) + ["xy"] * 2)
    small = halving.small
    pool = Pool(lsem)
    spend = halving.spend
    frame = halving.frame

    up = [lambda j=j: we.at[:, pl.ds(j * d, d)] for j in range(steps)]
    down = [lambda j=j: wr.at[pl.ds(j * d, d)] for j in range(steps)]
    own = [[lambda i=i, j=j: w_in.at[i, j] for j in range(3)] for i in range(2)]
    back = [lambda i=i: w_out.at[i] for i in range(2)]
    blocks = [*own[0], back[0], *own[1], back[1]]
    for j in range(steps + 1):
        blocks += up[j : j + 1] + (down[j - 1 : j] if j else [])
    for j in range(steps + 1):
        blocks += down[j : j + 1] + (up[j - 1 : j] if j else [])
    blocks += [back[1], *own[1], back[0], *own[0]]

    def swap(b):
        return halving.remote(
            memory.at[b, 0, 1 - frame], far_mem.at[b], (xsem.at[0, b], xsem.at[1, b]), halving.partners["xz"][0]
        )

    def attention_phase(tok, mem, a0, q, k, v, c, e, r_, mask):
        first = pool.start(tok_h, tok)
        stream = Stream(blocks, wbuf, wsem)
        halving.greet()
        own_mem = [pool.start(memory.at[b, 0, frame], mem.at[pl.ds(b * cols, half)]) for b in range(nb)]
        square = (rows, rows)
        causal = lax.broadcasted_iota(jnp.int32, square, 1) <= lax.broadcasted_iota(jnp.int32, square, 0)
        for b in range(nb):
            same = segments(tok_len, b, frame, square, 0) == segments(tok_len, b, frame, square, 1)
            mask[b] = jnp.where(same & causal, 0.0, -1e30)
        first.wait()
        n0, _ = stats(tok[...].astype(F32))
        a0[...] = (n0 * gain[0:1, :] + shift[0:1, :]).astype(BF)
        w = stream.take()
        q[...] = ((dot(a0[...], w[...]) + bias[0, 0:1, :]).astype(BF).astype(F32) * FACTOR).astype(BF)
        w = stream.take()
        k[...] = dot(a0[...], w[...]).astype(BF)
        w = stream.take()
        v[...] = (dot(a0[...], w[...]) + bias[1, 0:1, :]).astype(BF)
        stores = Group(pool)
        stores.start((a0, a0_h), (q, sq), (k, sk), (v, sv))
        halving.meet()
        for b in range(nb):
            swap(b).start()
        attend(nb, rows, rows, q, k, v, e, r_, c, mask)
        stores.start((e, se), (r_, sr), (c, sc))
        w = stream.take()
        dh[...] = tok[...].astype(F32) + dot(c[...], w[...]) + bias[2, 0:1, :]
        n1, _ = stats(dh[...])
        raw[...] = (n1 * gain[1:2, :] + shift[1:2, :]).astype(BF)
        kept = Group(pool)
        kept.start((dh, h1_h), (raw, a1_h))
        w = stream.take()
        dx[...] = ((dot(raw[...], w[...]) + bias[0, 1:2, :]).astype(BF).astype(F32) * FACTOR).astype(BF)
        kept.start((dx, cq_h))
        for x in own_mem:
            x.wait()
        for b in range(nb):
            swap(b).wait_recv()
        theirs = [pool.start(far_mem.at[b], mem.at[pl.ds(b * cols + half, half)]) for b in range(nb)]
        shape = (rows, cols)
        for b in range(nb):
            same = segments(tok_len, b, frame, shape, 0) == segments(frm_len, b, frame, shape, 1, frame * half)
            mask[b] = jnp.where(same, 0.0, -1e30)
        stores.wait(4)
        for x in theirs:
            x.wait()
        w = stream.take()
        k[...] = dot(mem[...], w[...]).astype(BF)
        w = stream.take()
        v[...] = (dot(mem[...], w[...]) + bias[1, 1:2, :]).astype(BF)
        stores.wait_all()
        stores.start((k, ck_h), (v, cv_h))
        attend(nb, rows, cols, dx, k, v, e, r_, c, mask)
        stores.start((e, ce), (r_, cr), (c, cc_h))
        kept.wait_all()
        w = stream.take()
        dh[...] += dot(c[...], w[...]) + bias[2, 1:2, :]
        n2, _ = stats(dh[...])
        raw[...] = (n2 * gain[2:3, :] + shift[2:3, :]).astype(BF)
        for b in range(nb):
            swap(b).wait_send()
        stores.wait_all()
        return stream.taken

    stream_at = []

    def run_attention(*scratch):
        stream_at.append(attention_phase(*scratch))

    pl.run_scoped(
        run_attention,
        *[pltpu.VMEM(act, BF), pltpu.VMEM(macts, BF)],
        *[pltpu.VMEM(act, BF)] * 5,
        pltpu.VMEM(se.shape, BF),
        pltpu.VMEM(act, F32),
        pltpu.VMEM((nb, rows, cols), F32),
    )

    class Rest(Stream):
        def __init__(self):
            self.blocks, self.buf, self.sems = blocks, wbuf, wsem
            self.depth, self.taken = wbuf.shape[0], stream_at[0]

    stream = Rest()

    def feed_phase(u, g, gat, cot, out):
        later = pool.start(cot_h, cot)
        kept = [pool.start(dh, h2_h), pool.start(raw, a2_h)]
        stores = {}
        for j in range(steps + 1):
            if j < steps:
                w = stream.take()
                x = dot(raw[...], w[...]) + eb[:, j * d : (j + 1) * d]
                if j >= 2:
                    stores[j - 2].wait()
                u[j % 2] = x.astype(BF)
                g[j % 2] = (0.5 * x * (1.0 + jnp.tanh(x * (GELU_C + GELU_D * (x * x))))).astype(BF)
                stores[j] = pool.start(u.at[j % 2], u_h.at[j])
            if j > 0:
                w = stream.take()
                y = dot(g[(j - 1) % 2], w[...])
                if j == 1:
                    for x in kept:
                        x.wait()
                    dh[...] += y + rb[...]
                else:
                    dh[...] += y
                gat[pl.ds((j - 1) * d, d), :] = g[(j - 1) % 2].T.astype(gat.dtype)
        later.wait()
        n3, r3 = stats(dh[...])
        out[...] = (n3 * gain[3:4, :] + shift[3:4, :]).astype(BF)
        stored = pool.start(out, out_o)
        e = cot[...].astype(F32)
        small[0] = jnp.zeros((SMALL_ROWS, d), F32)
        small[0, 9:10, :] = row_sum(e * n3)
        small[0, 13:14, :] = row_sum(e)
        eg = e * gain[3:4, :]
        dh[...] = r3 * (
            eg - jnp.mean(eg, axis=-1, keepdims=True) - n3 * jnp.mean(eg * n3, axis=-1, keepdims=True)
        )
        df[...] = dh[...].astype(BF)
        for i in range(4):
            gather(halving, r, i, 4, gat, perm)
            grad(halving, perm, df)
        small[0, 18:19, :] = row_sum(df[...])
        for j in range(max(0, steps - 2), steps):
            stores[j].wait()
        stored.wait()

    pl.run_scoped(
        feed_phase,
        pltpu.VMEM((2, t, d), BF),
        pltpu.VMEM((2, t, d), BF),
        pltpu.VMEM((steps * d, t), at.dtype),
        pltpu.VMEM(act, BF),
        pltpu.VMEM(act, BF),
    )

    def feed_back_phase(u, du, acc, h2):
        flight = [pool.start(u_h.at[j], u.at[j]) for j in range(2)]
        turned = pool.start(a2_h, raw)
        later = pool.start(h2_h, h2)
        for j in range(steps + 1):
            if j < steps:
                flight[j].wait()
                x = u[j % 2].astype(F32)
                x2 = x * x
                th = jnp.tanh(x * (GELU_C + GELU_D * x2))
                slope = (0.5 + 0.5 * th) * (1.0 + (1.0 - th) * (x * (GELU_C + (3 * GELU_D) * x2)))
                w = stream.take()
                y = dot_t(df[...], w[...]) * slope
                du[j] = y.astype(BF)
                small[0, 14 + j : 15 + j, :] = row_sum(y)
                if j + 2 < steps:
                    flight.append(pool.start(u_h.at[j + 2], u.at[j % 2]))
                spend(2.4)
            if j > 0:
                w = stream.take()
                z = dot_t(du[j - 1], w[...])
                if j == 1:
                    acc[...] = z
                else:
                    acc[...] += z
                spend(1.6)
                if j == 1:
                    turned.wait()
                    turn(halving, r, raw, at, perm)
                grad(halving, perm, du.at[j - 1])
        turned = pool.start(cc_h, raw)
        later.wait()
        back_, small[0, 8:9, :], small[0, 12:13, :] = norm_back(acc[...], h2[...], gain[2:3, :])
        dh[...] += back_
        dx[...] = dh[...].astype(BF)
        small[0, 5:6, :] = row_sum(dx[...])
        spend(1.2)
        w = stream.take()
        dc[...] = dot_t(dx[...], w[...]).astype(BF)
        spend(1.3)
        turned.wait()
        turn(halving, r, raw, at, perm)
        grad(halving, perm, dx)

    pl.run_scoped(
        feed_back_phase,
        pltpu.VMEM((2, t, d), BF),
        pltpu.VMEM((steps, t, d), BF),
        pltpu.VMEM(act, F32),
        pltpu.VMEM(act, F32),
    )

    def cross_back_phase(e, r_, q, k, v, c, dq, dk, dv, gm):
        loads = Group(pool)
        start_parts(loads, nb, ce, e, (cr, r_), (cc_h, c), (cv_h, v), (ck_h, k), (cq_h, q))
        turned = pool.start(a1_h, raw)
        later = pool.start(h1_h, gm)
        for i in range(PARTS):
            loads.wait(6)
            attend_back(nb, rows, cols, i, e, r_, q, k, v, c, dc, dq, dk, dv)
            spend(2.2)
        turned.wait()
        turn(halving, r, raw, at, perm)
        turned = Group(pool)
        for b in range(nb):
            turned.start(
                (memory.at[b, 0, frame], raw.at[pl.ds(b * cols, half)]),
                (far_mem.at[b], raw.at[pl.ds(b * cols + half, half)]),
            )
        grad(halving, perm, dq)
        w = stream.take()
        up_ = dot_t(dq[...], w[...])
        later.wait()
        back_, small[0, 7:8, :], small[0, 11:12, :] = norm_back(up_, gm[...], gain[1:2, :])
        dh[...] += back_
        dx[...] = dh[...].astype(BF)
        small[0, 2:3, :] = row_sum(dx[...])
        small[0, 3:4, :] = row_sum(dq[...])
        small[0, 4:5, :] = row_sum(dv[...])
        spend(2.6)
        turned.wait_all()
        turn(halving, r, raw, at, perm)
        turned = pool.start(sc, raw)
        grad(halving, perm, dk)
        grad(halving, perm, dv)
        w = stream.take()
        gm[...] = dot_t(dk[...], w[...])
        w = stream.take()
        gm[...] += dot_t(dv[...], w[...])
        spend(2.6)
        moves = []
        for b in range(nb):
            moves.append(pool.start(gm.at[pl.ds(b * cols, half)], gm_o.at[b, 0, frame]))
            far = halving.remote(
                gm.at[pl.ds(b * cols + half, half)], gm_o.at[b, 0, frame],
                (xsem.at[0, nb + b], xsem.at[1, nb + b]), halving.partners["xz"][0],
            )
            far.start()
            moves.append(far)
        w = stream.take()
        dc[...] = dot_t(dx[...], w[...]).astype(BF)
        spend(1.3)
        turned.wait()
        turn(halving, r, raw, at, perm)
        grad(halving, perm, dx)
        for x in moves:
            x.wait()

    pl.run_scoped(
        cross_back_phase,
        pltpu.VMEM(ce.shape, BF),
        pltpu.VMEM(act, F32),
        pltpu.VMEM(act, BF),
        pltpu.VMEM(macts, BF),
        pltpu.VMEM(macts, BF),
        pltpu.VMEM(act, BF),
        pltpu.VMEM(act, BF),
        pltpu.VMEM(macts, BF),
        pltpu.VMEM(macts, BF),
        pltpu.VMEM(macts, F32),
    )

    def self_back_phase(e, r_, q, k, v, c, dq, dk, dv, tok):
        loads = Group(pool)
        start_parts(loads, nb, se, e, (sr, r_), (sc, c), (sv, v), (sk, k), (sq, q))
        turned = pool.start(a0_h, raw)
        later = pool.start(tok_h, tok)
        for i in range(PARTS):
            loads.wait(6)
            attend_back(nb, rows, rows, i, e, r_, q, k, v, c, dc, dq, dk, dv)
            spend(2.2)
        turned.wait()
        turn(halving, r, raw, at, perm)
        grad(halving, perm, dq)
        gather(halving, r, 0, 1, at, perm)
        grad(halving, perm, dk)
        grad(halving, perm, dv)
        w = stream.take()
        up_ = dot_t(dq[...], w[...])
        w = stream.take()
        up_ += dot_t(dk[...], w[...])
        w = stream.take()
        up_ += dot_t(dv[...], w[...])
        later.wait()
        back_, small[0, 6:7, :], small[0, 10:11, :] = norm_back(up_, tok[...].astype(F32), gain[0:1, :])
        dh[...] += back_
        moved = pool.start(dh, gt_o)
        small[0, 0:1, :] = row_sum(dq[...])
        small[0, 1:2, :] = row_sum(dv[...])
        halving.small_start()
        spend(5.2)
        moved.wait()

    pl.run_scoped(self_back_phase, pltpu.VMEM(se.shape, BF), pltpu.VMEM(act, F32), *[pltpu.VMEM(act, BF)] * 8)
    halving.finish()
    done = pltpu.make_async_copy(small.at[halving.stages + 1], small_o, osem)
    done.start()
    done.wait()


def layer(n_dp, nb, tok_len, frm_len, bias, gain, shift, rb, eb, tok, memory, cot, w_in, w_out, we, wr):
    t, d = tok.shape
    ff = we.shape[1]
    n = 2 * n_dp
    r = d // n
    rows, half = t // nb, memory.shape[3]
    m = 2 * half * nb
    kind = BF if r % 16 == 0 else F32
    act, macts = (t, d), (m, d)
    sem = pltpu.SemaphoreType.DMA
    held = [hbm((nb, half, d), BF), hbm(act, F32), hbm(act, F32), hbm(act, F32), hbm(act, F32)]
    held += [hbm((nb, HEADS, rows, rows), BF), hbm((nb, HEADS, rows, 2 * half), BF), hbm((ff // d, t, d), BF)]
    held += [hbm(act, BF)] * 7 + [hbm(macts, BF)] * 2 + [hbm(act, BF)] * 2
    assert len(held) == HELD + 1
    return pl.pallas_call(
        functools.partial(layer_kernel, n_dp, nb),
        out_shape=[
            hbm(act, BF), hbm((4 * r, d), F32), hbm((r, ff), F32), hbm((2, 3, r, d), F32), hbm((2, r, d), F32),
            hbm((SMALL_ROWS, d), F32), hbm(act, F32), hbm(memory.shape, F32),
        ]
        + held,
        in_specs=[SM] * 2 + [VM] * 5 + [ANY] * 7,
        out_specs=[ANY] * (8 + len(held)),
        scratch_shapes=halving_scratch(n_dp, d, UNITS)
        + [
            pltpu.VMEM((4, d, d), BF),
            pltpu.VMEM(act, BF),
            pltpu.VMEM(act, F32),
            *[pltpu.VMEM(act, BF)] * 3,
            pltpu.VMEM((d, t), kind),
            pltpu.VMEM((d, t), BF),
            sem((15 + 4 * (ff // d) + 8,)),
            sem((160,)),
            sem((2, 2 * nb)),
            sem,
        ],
        compiler_params=pltpu.CompilerParams(vmem_limit_bytes=63 * 2**20, collective_id=0, has_side_effects=True),
        name="layer",
    )(tok_len, frm_len, bias, gain, shift, rb, eb, tok, memory, cot, w_in, w_out, we, wr)[:8]


def finish_kernel(n, count, small, *refs):
    ins, outs = refs[:count], refs[count : 2 * count]
    bias, gain, shift, eb, rb = refs[2 * count : 2 * count + 5]
    bufs = refs[2 * count + 5 : -2]
    loads, stores = Copies(refs[-2]), Copies(refs[-1])
    loads.start(*zip(ins, bufs))
    me = 2 * lax.axis_index("dp") + lax.axis_index("frame")
    d = small.shape[1]
    w, wide = bias.shape[2], eb.shape[1]

    def window(rows, first, width):
        return pltpu.roll(rows, d - first, 1)[:, :width]

    mine = window(small[...], me * w, w)
    for i in range(3):
        bias[i] = jnp.concatenate([mine[i : i + 1], mine[3 + i : 4 + i]], axis=0)
    gain[...], shift[...] = mine[6:10], mine[10:14]
    rb[...] = mine[18:19]
    place = me * wide
    row = small[14:15, :]
    for i in range(1, n * wide // d):
        row = jnp.where(place // d == i, small[14 + i : 15 + i, :], row)
    eb[...] = window(row, place % d, wide)
    for buf, out in zip(bufs, outs):
        loads.wait()
        stores.start((buf, out))
    stores.wait_all()


def finish(n, ff, small, *arrays):
    d = small.shape[1]
    w = d // n
    count = len(arrays)
    return pl.pallas_call(
        functools.partial(finish_kernel, n, count),
        out_shape=[hbm(x.shape, x.dtype) for x in arrays]
        + [hbm((3, 2, w), F32), hbm((4, w), F32), hbm((4, w), F32), hbm((1, ff // n), F32), hbm((1, w), F32)],
        in_specs=[VM] + [ANY] * count,
        out_specs=[ANY] * count + [VM] * 5,
        scratch_shapes=[pltpu.VMEM(x.shape, x.dtype) for x in arrays] + [pltpu.SemaphoreType.DMA((count,))] * 2,
        compiler_params=params(),
        name="finish",
    )(small, *arrays)


def local(
    n_dp,
    tokens,
    memory,
    token_lengths,
    frame_lengths,
    attention_in,
    attention_out,
    attention_bias,
    norm_gain,
    norm_bias,
    expand_weight,
    expand_bias,
    reduce_weight,
    reduce_bias,
    cotangent,
):
    n = 2 * n_dp
    nb = tokens.shape[0]
    t = nb * tokens.shape[3]
    ff = expand_weight.shape[1]
    out, grad_reduce, grad_expand, grad_in, grad_out, small, grad_tokens, grad_memory = layer(
        n_dp, nb, token_lengths, frame_lengths, jnp.transpose(attention_bias, (1, 0, 2)), norm_gain, norm_bias,
        reduce_bias.reshape(1, D), expand_bias.reshape(1, ff), tokens.reshape(t, D), memory,
        cotangent.reshape(t, D), attention_in, attention_out, expand_weight, reduce_weight,
    )
    out, grad_tokens, grad_memory, grad_reduce, grad_expand, grad_in, grad_out, *rest = finish(
        n, ff, small, out, grad_tokens, grad_memory, grad_reduce, grad_expand, grad_in, grad_out
    )
    grad_bias, grad_gain, grad_shift, grad_eb, grad_rb = rest
    shape = tokens.shape
    return (
        out.reshape(shape),
        grad_tokens.reshape(shape),
        grad_memory,
        grad_in,
        grad_out,
        jnp.transpose(grad_bias, (1, 0, 2)),
        grad_gain,
        grad_shift,
        grad_expand,
        grad_eb.reshape(-1),
        grad_reduce,
        grad_rb.reshape(-1),
    )


def solution(mesh):
    spread = P(None, "dp", "frame", None, None)
    by_frame = P(None, "dp", None, "frame", None)
    both = ("dp", "frame")
    lengths = P(None, "dp", None, None)
    return jax.shard_map(
        functools.partial(local, mesh.shape["dp"]),
        mesh=mesh,
        in_specs=(spread, by_frame, lengths, lengths) + (P(),) * 9 + (spread,),
        out_specs=(
            spread,
            spread,
            by_frame,
            P(None, None, both, None),
            P(None, both, None),
            P(None, None, both),
            P(None, both),
            P(None, both),
            P(both, None),
            P(both),
            P(both, None),
            P(both),
        ),
        check_vma=False,
    )
```

```python
import functools
import math

import jax
import jax.numpy as jnp
from jax import lax
from jax.experimental import pallas as pl
from jax.experimental.pallas import tpu as pltpu
from jax.sharding import PartitionSpec as P

D = 1024
HEADS = 16
HEAD_DIM = 64
FACTOR = 1.0 / math.sqrt(HEAD_DIM)
BF = jnp.bfloat16
F32 = jnp.float32


def dot(a, b):
    return jnp.dot(a, b, preferred_element_type=F32)


def dot_t(a, b):
    return lax.dot_general(a, b, (((1,), (1,)), ((), ())), preferred_element_type=F32)


VM = pl.BlockSpec(memory_space=pltpu.VMEM)
SM = pl.BlockSpec(memory_space=pltpu.SMEM)
ANY = pl.BlockSpec(memory_space=pl.ANY)
GELU_C = 0.7978845608028654
GELU_D = 0.044715 * GELU_C


def params(mib=58):
    return pltpu.CompilerParams(vmem_limit_bytes=mib * 2**20)


def hbm(shape, kind):
    return jax.ShapeDtypeStruct(shape, kind)


class Copies:
    def __init__(self, sems):
        self.sems, self.copies, self.done = sems, [], 0

    def start(self, *pairs):
        for src, dst in pairs:
            copy = pltpu.make_async_copy(src, dst, self.sems.at[len(self.copies)])
            copy.start()
            self.copies.append(copy)

    def wait(self, count=1):
        for copy in self.copies[self.done : self.done + count]:
            copy.wait()
        self.done += count

    def wait_all(self):
        self.wait(len(self.copies) - self.done)


def stats(v):
    off = v - jnp.mean(v, axis=-1, keepdims=True)
    r = lax.rsqrt(jnp.mean(off * off, axis=-1, keepdims=True) + 1e-5)
    return off * r, r


def norm_back(e, v, gain):
    n, r = stats(v)
    eg = e * gain
    back = r * (
        eg - jnp.mean(eg, axis=-1, keepdims=True) - n * jnp.mean(eg * n, axis=-1, keepdims=True)
    )
    return back, row_sum(e * n), row_sum(e)


def row_sum(x):
    return jnp.sum(x.astype(F32), axis=0, keepdims=True)


def pair_mask(rows):
    return lax.broadcasted_iota(jnp.int32, (rows, 128), 1) < HEAD_DIM


def segments(lengths, b, a, shape, dim, shift=0):
    pos = lax.broadcasted_iota(jnp.int32, shape, dim) + shift
    pos = jnp.where(pos >= shape[dim], pos - shape[dim], pos)
    total, seg = 0, jnp.zeros(shape, jnp.int32)
    for i in range(lengths.shape[3] - 1):
        total = total + lengths[b, 0, a, i]
        seg = seg + (pos >= total).astype(jnp.int32)
    return seg


def attend(nb, rows, cols, part, q, k, v, e_ref, r_ref, c, mask):
    low = pair_mask(rows)
    one = jnp.ones((cols, 128), BF)

    for j in range(part * HEADS // 4, (part + 1) * HEADS // 4):
        lanes = pl.ds(j * 128, 128)
        for b in range(nb):
            qs, ks = pl.ds(b * rows, rows), pl.ds(b * cols, cols)
            q2, k2, v2 = q[qs, lanes], k[ks, lanes], v[ks, lanes]
            zero = jnp.zeros_like(q2)
            both = jnp.concatenate([jnp.where(low, q2, zero), jnp.where(low, zero, q2)], axis=0)
            s = dot_t(both, k2).reshape(2, rows, cols) + mask[b][None]
            e = jnp.exp(s - jnp.max(s, axis=-1, keepdims=True)).astype(BF)
            e_ref[b, pl.ds(2 * j, 2)] = e
            o = dot(e.reshape(2 * rows, cols), jnp.concatenate([v2, one], axis=1))
            r = 1.0 / jnp.where(low, o[:rows, 128:], o[rows:, 128:])
            r_ref[qs, lanes] = r
            c[qs, lanes] = (jnp.where(low, o[:rows, :128], o[rows:, :128]) * r).astype(BF)


def attend_back(nb, rows, cols, part, e_ref, r_ref, q, k, v, c, dc, dq, dk, dv):
    low, low_k = pair_mask(rows), pair_mask(cols)
    minus = jnp.full((cols, 128), -1, BF)

    count = HEADS // 2 // PARTS
    for j in range(part * count, (part + 1) * count):
        lanes = pl.ds(j * 128, 128)
        for b in range(nb):
            qs, ks = pl.ds(b * rows, rows), pl.ds(b * cols, cols)
            q2, k2, v2 = q[qs, lanes], k[ks, lanes], v[ks, lanes]
            dcs = dc[qs, lanes].astype(F32) * r_ref[qs, lanes]
            delta = (dcs * c[qs, lanes].astype(F32)).astype(BF)
            dcs = dcs.astype(BF)
            zero = jnp.zeros_like(dcs)
            first = jnp.concatenate([jnp.where(low, dcs, zero), jnp.where(low, delta, zero)], axis=1)
            second = jnp.concatenate([jnp.where(low, zero, dcs), jnp.where(low, zero, delta)], axis=1)
            slope = dot_t(
                jnp.concatenate([first, second], axis=0), jnp.concatenate([v2, minus], axis=1)
            )
            e = e_ref[b, pl.ds(2 * j, 2)]
            ds = (e.astype(F32) * slope.reshape(2, rows, cols)).astype(BF)
            g = dot(ds.reshape(2 * rows, cols), k2)
            dq[qs, lanes] = (jnp.where(low, g[:rows], g[rows:]) * FACTOR).astype(BF)
            g = dot(jnp.concatenate([ds[0].T, ds[1].T], axis=0), q2)
            dk[ks, lanes] = jnp.where(low_k, g[:cols], g[cols:]).astype(BF)
            g = dot(jnp.concatenate([e[0].T, e[1].T], axis=0), dcs)
            dv[ks, lanes] = jnp.where(low_k, g[:cols], g[cols:]).astype(BF)


PARTS = 4


def start_parts(loads, nb, e_h, e, *pairs):
    for i in range(PARTS):
        heads = pl.ds(i * HEADS // PARTS, HEADS // PARTS)
        loads.start((e_h.at[:, heads], e.at[:, heads]))
        for src, dst in pairs:
            lanes = pl.ds(i * (D // PARTS), D // PARTS)
            loads.start((src.at[:, lanes], dst.at[:, lanes]))


K_SLOTS = 9
R_SLOTS = 6
S_SLOTS = 4
C_SLOTS = 4
F_SLOTS = 4
PERIOD = 6.3
START = 2.0


ORDERS = {
    "xz": ([0, 2, 1, 3], [1, 2, 0, 3]),
    "zx": ([2, 0, 1, 3], [2, 1, 0, 3]),
    "xy": ([0, 1, 2, 3], [1, 0, 2, 3]),
}


def stage_masks(n_dp, order):
    m = n_dp.bit_length() - 1
    if m == 4:
        orders = ORDERS[order]
    else:
        one = list(range(0, m, 2)) + list(range(1, m, 2))
        orders = one, one[1:] + one[:1]
    return [(1 << a, 1 << b) for a, b in zip(*orders)]


def place_masks(n_dp, order):
    masks = stage_masks(n_dp, order)
    m = len(masks)
    out = []
    for f in range(2):
        row = []
        for p in range(2 * n_dp):
            far = p >> m
            mask = far
            for s in range(m):
                if (p >> (m - 1 - s)) & 1:
                    mask ^= 2 * masks[s][1 - f if far else f]
            row.append(mask)
        out.append(row)
    return out


def shard_at(n_dp, order, dp, frame, p):
    masks = place_masks(n_dp, order)
    mine = total = 2 * dp + frame
    step = 1
    while step < 2 * n_dp:
        zero, one = (masks[0][p] // step) % 2, (masks[1][p] // step) % 2
        if zero or one:
            flips = step if zero == one else step * (zero + frame * (one - zero))
            total = total + flips * (1 - 2 * ((mine // step) % 2))
        step *= 2
    return total


class Halving:
    def __init__(self, n_dp, refs, outs, orders):
        self.n_dp, self.outs = n_dp, outs
        self.widths = [out.shape[1] for out in outs]
        self.units = len(outs)
        self.s, self.r0, self.k, self.r, self.kf, self.rf, self.fin = refs[:7]
        self.small, self.small_r, self.sems, self.small_sems, self.fin_sem = refs[7:]
        self.orders = orders
        self.stages = n_dp.bit_length() - 1
        self.lags = [0, 2, 4] + [stage + 2 for stage in range(3, self.stages + 1)]
        self.dp, self.frame = lax.axis_index("dp"), lax.axis_index("frame")
        self.partners = {
            order: [(self.dp, 1 - self.frame)] + [(self.flip(m), self.frame) for m in stage_masks(n_dp, order)]
            for order in ORDERS
        }
        self.started, self.waited, self.stored = [], set(), set()
        self.now, self.slot, self.made, self.core, self.ended = 0.0, 0, 0, 0, 0
        self.small_step = None

    def flip(self, mask):
        bit = mask[0] + self.frame * (mask[1] - mask[0])
        return self.dp + bit * (1 - 2 * ((self.dp // bit) % 2))

    def greet(self):
        barrier = pltpu.get_barrier_semaphore()
        for stage in range(self.stages + 1):
            pl.semaphore_signal(
                barrier, inc=1, device_id=self.partners["xz"][stage], device_id_type=pl.DeviceIdType.MESH
            )

    def meet(self):
        pl.semaphore_wait(pltpu.get_barrier_semaphore(), self.stages + 1)

    def rows(self, stage):
        return self.s.shape[1] >> stage

    def wide(self, stage):
        return stage > 0 and self.rows(stage) < 16

    def remote(self, src, dst, sems, partner):
        return pltpu.make_async_remote_copy(
            src_ref=src, dst_ref=dst, send_sem=sems[0], recv_sem=sems[1],
            device_id=partner, device_id_type=pl.DeviceIdType.MESH,
        )

    def copy(self, c, stage):
        h = self.rows(stage)
        half = pl.ds(h, h)
        if c is None:
            src, dst = self.small.at[stage], self.small_r.at[stage]
            sems = self.small_sems.at[0, stage], self.small_sems.at[1, stage]
        else:
            sems = self.sems.at[0, c, stage], self.sems.at[1, c, stage]
            lanes = pl.ds(0, self.widths[c])
            if stage == 0:
                src, dst = self.s.at[c % S_SLOTS, :, lanes], self.r0.at[c % C_SLOTS, :, lanes]
            elif self.wide(stage):
                src, dst = self.kf.at[c % K_SLOTS, half, lanes], self.rf.at[c % R_SLOTS, half, lanes]
            else:
                src, dst = self.k.at[c % K_SLOTS, half, lanes], self.r.at[c % R_SLOTS, half, lanes]
        return self.remote(src, dst, sems, self.partners["xz" if c is None else self.orders[c]][stage])

    def send(self, c, stage):
        self.started.append((c, stage))
        self.copy(c, stage).start()

    def sent(self, c, stage):
        if (c, stage) not in self.waited:
            self.waited.add((c, stage))
            self.copy(c, stage).wait_send()

    def store(self, c):
        return pltpu.make_async_copy(
            self.fin.at[c % F_SLOTS, :, pl.ds(0, self.widths[c])], self.outs[c], self.fin_sem.at[c]
        )

    def free(self, c):
        while self.core < c - 1:
            self.join()
        if c >= S_SLOTS:
            self.sent(c - S_SLOTS, 0)
        if c >= K_SLOTS:
            while self.ended <= c - K_SLOTS:
                self.step()
            for stage in range(1, self.stages + 1):
                self.sent(c - K_SLOTS, stage)

    def join(self):
        c = self.core
        assert c < self.made
        self.copy(c, 0).wait_recv()
        slot, lanes = c % K_SLOTS, pl.ds(0, self.widths[c])
        own, got = self.k[slot, :, lanes], self.r0[c % C_SLOTS, :, lanes]
        self.k[slot, :, lanes] = (own.astype(F32) + got.astype(F32)).astype(BF)
        self.core += 1
        self.now += 0.4

    def fold(self, c, stage):
        h = self.rows(stage)
        near, half = pl.ds(0, h), pl.ds(h, h)
        slot, slot_r, lanes = c % K_SLOTS, c % R_SLOTS, pl.ds(0, self.widths[c])
        self.copy(c, stage).wait_recv()
        if self.wide(stage):
            total = self.kf[slot, near, lanes] + self.rf[slot_r, half, lanes]
        else:
            total = self.k[slot, near, lanes].astype(F32) + self.r[slot_r, half, lanes].astype(F32)
        if stage == self.stages:
            if c >= F_SLOTS:
                self.stored.add(c - F_SLOTS)
                self.store(c - F_SLOTS).wait()
            self.fin[c % F_SLOTS, :, lanes] = total
            self.store(c).start()
            self.ended = c + 1
            return
        if self.wide(stage + 1):
            self.kf[slot, near, lanes] = total
        else:
            self.k[slot, near, lanes] = total.astype(BF)
        self.send(c, stage + 1)

    def small_start(self):
        self.small_step = 0
        self.send(None, 0)

    def step(self):
        k = self.slot
        self.slot += 1
        if k < self.units:
            while self.core <= k:
                self.join()
            self.send(k, 1)
        for stage in range(1, self.stages + 1):
            c = k - self.lags[stage]
            if 0 <= c < self.units:
                self.fold(c, stage)
                self.now += 0.25
        self.small_fold()

    def small_fold(self):
        stage = self.small_step
        if stage is None or stage > self.stages:
            return
        self.copy(None, stage).wait_recv()
        self.small[stage + 1] = self.small[stage] + self.small_r[stage]
        self.small_step += 1
        if stage < self.stages:
            self.send(None, stage + 1)

    def spend(self, us):
        self.now += us
        while self.slot < self.made and START + PERIOD * sum(self.widths[: self.slot]) / D <= self.now:
            self.step()

    def finish(self):
        while self.ended < self.units:
            self.step()
        while self.small_step <= self.stages:
            self.small_fold()
        for c, stage in self.started:
            self.sent(c, stage)
        for c in range(self.units):
            if c not in self.stored:
                self.store(c).wait()


def halving_scratch(n_dp, d, units):
    n = 2 * n_dp
    m = d // 2
    stages = n_dp.bit_length() - 1
    sem = pltpu.SemaphoreType.DMA
    wide = (m >> stages) < 16
    return [
        pltpu.VMEM((S_SLOTS, m, d), BF),
        pltpu.VMEM((C_SLOTS, m, d), BF),
        pltpu.VMEM((K_SLOTS, m, d), BF),
        pltpu.VMEM((R_SLOTS, m, d), BF),
        pltpu.VMEM((K_SLOTS, 16, d) if wide else (1, 8, 128), F32),
        pltpu.VMEM((R_SLOTS, 16, d) if wide else (1, 8, 128), F32),
        pltpu.VMEM((F_SLOTS, d // n, d), F32),
        pltpu.VMEM((stages + 2, 24, d), F32),
        pltpu.VMEM((stages + 1, 24, d), F32),
        sem((2, units, stages + 1)),
        sem((2, stages + 1)),
        sem((units,)),
    ]


class Pool:
    def __init__(self, sems):
        self.sems, self.used = sems, 0

    def start(self, src, dst):
        copy = pltpu.make_async_copy(src, dst, self.sems.at[self.used])
        self.used += 1
        copy.start()
        return copy


class Group:
    def __init__(self, pool):
        self.pool, self.copies, self.done = pool, [], 0

    def start(self, *pairs):
        for src, dst in pairs:
            self.copies.append(self.pool.start(src, dst))

    def wait(self, count):
        for copy in self.copies[self.done : self.done + count]:
            copy.wait()
        self.done += count

    def wait_all(self):
        self.wait(len(self.copies) - self.done)


class Stream:
    def __init__(self, blocks, buf, sems):
        self.blocks, self.buf, self.sems = blocks, buf, sems
        self.depth, self.taken = buf.shape[0], 0
        for i in range(self.depth - 1):
            self.copy(i).start()

    def copy(self, i):
        return pltpu.make_async_copy(self.blocks[i](), self.buf.at[i % self.depth], self.sems.at[i])

    def take(self):
        i = self.taken
        self.taken += 1
        ahead = i + self.depth - 2
        if i > 0 and ahead < len(self.blocks):
            if ahead >= self.depth - 1:
                self.copy(ahead).start()
        self.copy(i).wait()
        return self.buf.at[i % self.depth]


def store_half(stores, part, heads, *pairs):
    some = pl.ds(part * HEADS // 2, HEADS // 2)
    stores.start((heads[0].at[:, some], heads[1].at[:, some]))
    lanes = pl.ds(part * D // 2, D // 2)
    for src, dst in pairs:
        stores.start((src.at[:, lanes], dst.at[:, lanes]))


def turn(halving, r, src, at, perm):
    at[...] = src[...].T.astype(at.dtype)
    gather(halving, r, 0, 1, at, perm)


def gather(halving, r, u, count, at, perm):
    order = halving.orders[halving.made]
    for p in range(2 * halving.n_dp):
        base = shard_at(halving.n_dp, order, halving.dp, halving.frame, p) * (r * count)
        perm[pl.ds(p * r, r), :] = at[pl.ds(pl.multiple_of(base + u * r, 8), r), :].astype(perm.dtype)
    halving.spend(0.5)


def grad(halving, left, right):
    c = halving.made
    m = left.shape[0] // 2
    wide = right.shape[1]
    lanes = pl.ds(0, wide)
    assert wide == halving.widths[c]
    halving.free(c)
    halving.s[c % S_SLOTS, :, lanes] = dot(left[pl.ds(m, m), :], right[...]).astype(BF)
    halving.send(c, 0)
    halving.k[c % K_SLOTS, :, lanes] = dot(left[pl.ds(0, m), :], right[...]).astype(BF)
    halving.made += 1
    halving.spend(1.4 * wide / D)


SMALL_ROWS = 24
UNITS = 16
HELD = 18


def layer_kernel(n_dp, nb, *refs):
    (
        tok_len, frm_len, bias, gain, shift, rb, eb,
        tok_h, memory, cot_h, w_in, w_out, we, wr,
    ) = refs[:14]
    out_o, red_o, exp_o, in_o, out_w, small_o, gt_o, gm_o = refs[14:22]
    (
        far_mem, h1_h, h2_h, sr, cr, se, ce, u_h, sq, sk, sv, sc, a0_h, a1_h, cq_h, ck_h, cv_h, cc_h,
    ) = refs[22 : 22 + HELD]
    a2_h = refs[22 + HELD]
    rest = refs[23 + HELD :]
    hrefs = rest[:12]
    wbuf, df, dh, dx, dc, raw, at, perm, wsem, lsem, xsem, osem = rest[12:]
    t, d = df.shape
    steps = we.shape[1] // d
    r = d // (2 * n_dp)
    rows = t // nb
    half = memory.shape[3]
    cols = 2 * half
    act, macts = (t, d), (nb * cols, d)
    outs = [red_o.at[pl.ds(u * r, r)] for u in range(4)]
    outs += [exp_o.at[:, pl.ds(u * d, d)] for u in range(4)]
    outs += [out_w.at[1], in_o.at[1, 0], in_o.at[1, 1], in_o.at[1, 2]]
    outs += [out_w.at[0], in_o.at[0, 0], in_o.at[0, 1], in_o.at[0, 2]]
    halving = Halving(n_dp, hrefs, outs, ["xz"] * (UNITS - 2) + ["xy"] * 2)
    small = halving.small
    pool = Pool(lsem)
    spend = halving.spend
    frame = halving.frame

    up = [lambda j=j: we.at[:, pl.ds(j * d, d)] for j in range(steps)]
    down = [lambda j=j: wr.at[pl.ds(j * d, d)] for j in range(steps)]
    own = [[lambda i=i, j=j: w_in.at[i, j] for j in range(3)] for i in range(2)]
    back = [lambda i=i: w_out.at[i] for i in range(2)]
    blocks = [*own[0], back[0], *own[1], back[1]]
    for j in range(steps + 1):
        blocks += up[j : j + 1] + (down[j - 1 : j] if j else [])
    for j in range(steps + 1):
        blocks += down[j : j + 1] + (up[j - 1 : j] if j else [])
    blocks += [back[1], *own[1], back[0], *own[0]]

    def swap(b):
        return halving.remote(
            memory.at[b, 0, 1 - frame], far_mem.at[b], (xsem.at[0, b], xsem.at[1, b]), halving.partners["xz"][0]
        )

    def attention_phase(tok, mem, a0, q, k, v, c, e, r_, mask):
        first = pool.start(tok_h, tok)
        stream = Stream(blocks, wbuf, wsem)
        halving.greet()
        own_mem = [pool.start(memory.at[b, 0, frame], mem.at[pl.ds(b * cols, half)]) for b in range(nb)]
        square = (rows, rows)
        causal = lax.broadcasted_iota(jnp.int32, square, 1) <= lax.broadcasted_iota(jnp.int32, square, 0)
        for b in range(nb):
            same = segments(tok_len, b, frame, square, 0) == segments(tok_len, b, frame, square, 1)
            mask[b] = jnp.where(same & causal, 0.0, -1e30)
        first.wait()
        n0, _ = stats(tok[...].astype(F32))
        a0[...] = (n0 * gain[0:1, :] + shift[0:1, :]).astype(BF)
        w = stream.take()
        q[...] = ((dot(a0[...], w[...]) + bias[0, 0:1, :]).astype(BF).astype(F32) * FACTOR).astype(BF)
        w = stream.take()
        k[...] = dot(a0[...], w[...]).astype(BF)
        w = stream.take()
        v[...] = (dot(a0[...], w[...]) + bias[1, 0:1, :]).astype(BF)
        stores = Group(pool)
        stores.start((a0, a0_h), (q, sq), (k, sk), (v, sv))
        halving.meet()
        for b in range(nb):
            swap(b).start()
        for i in range(2):
            attend(nb, rows, rows, i, q, k, v, e, r_, c, mask)
            store_half(stores, i, (e, se), (r_, sr), (c, sc))
        w = stream.take()
        dh[...] = tok[...].astype(F32) + dot(c[...], w[...]) + bias[2, 0:1, :]
        n1, _ = stats(dh[...])
        raw[...] = (n1 * gain[1:2, :] + shift[1:2, :]).astype(BF)
        kept = Group(pool)
        kept.start((dh, h1_h), (raw, a1_h))
        for b in range(nb):
            swap(b).wait_recv()
        theirs = [pool.start(far_mem.at[b], mem.at[pl.ds(b * cols + half, half)]) for b in range(nb)]
        w = stream.take()
        dx[...] = ((dot(raw[...], w[...]) + bias[0, 1:2, :]).astype(BF).astype(F32) * FACTOR).astype(BF)
        kept.start((dx, cq_h))
        for x in own_mem:
            x.wait()
        shape = (rows, cols)
        for b in range(nb):
            same = segments(tok_len, b, frame, shape, 0) == segments(frm_len, b, frame, shape, 1, frame * half)
            mask[b] = jnp.where(same, 0.0, -1e30)
        stores.wait(4)
        for x in theirs:
            x.wait()
        w = stream.take()
        k[...] = dot(mem[...], w[...]).astype(BF)
        w = stream.take()
        v[...] = (dot(mem[...], w[...]) + bias[1, 1:2, :]).astype(BF)
        stores.wait_all()
        stores.start((k, ck_h), (v, cv_h))
        for i in range(2):
            attend(nb, rows, cols, i, dx, k, v, e, r_, c, mask)
            store_half(stores, i, (e, ce), (r_, cr), (c, cc_h))
        kept.wait_all()
        w = stream.take()
        dh[...] += dot(c[...], w[...]) + bias[2, 1:2, :]
        n2, _ = stats(dh[...])
        raw[...] = (n2 * gain[2:3, :] + shift[2:3, :]).astype(BF)
        for b in range(nb):
            swap(b).wait_send()
        stores.wait_all()
        return stream.taken

    stream_at = []

    def run_attention(*scratch):
        stream_at.append(attention_phase(*scratch))

    pl.run_scoped(
        run_attention,
        *[pltpu.VMEM(act, BF), pltpu.VMEM(macts, BF)],
        *[pltpu.VMEM(act, BF)] * 5,
        pltpu.VMEM(se.shape, BF),
        pltpu.VMEM(act, F32),
        pltpu.VMEM((nb, rows, cols), F32),
    )

    class Rest(Stream):
        def __init__(self):
            self.blocks, self.buf, self.sems = blocks, wbuf, wsem
            self.depth, self.taken = wbuf.shape[0], stream_at[0]

    stream = Rest()

    def feed_phase(u, g, gat, cot, out):
        later = pool.start(cot_h, cot)
        kept = [pool.start(dh, h2_h), pool.start(raw, a2_h)]
        stores = {}
        for j in range(steps + 1):
            if j < steps:
                w = stream.take()
                x = dot(raw[...], w[...]) + eb[:, j * d : (j + 1) * d]
                if j >= 2:
                    stores[j - 2].wait()
                u[j % 2] = x.astype(BF)
                g[j % 2] = (0.5 * x * (1.0 + jnp.tanh(x * (GELU_C + GELU_D * (x * x))))).astype(BF)
                stores[j] = pool.start(u.at[j % 2], u_h.at[j])
            if j > 0:
                w = stream.take()
                y = dot(g[(j - 1) % 2], w[...])
                if j == 1:
                    for x in kept:
                        x.wait()
                    dh[...] += y + rb[...]
                else:
                    dh[...] += y
                gat[pl.ds((j - 1) * d, d), :] = g[(j - 1) % 2].T.astype(gat.dtype)
        later.wait()
        n3, r3 = stats(dh[...])
        out[...] = (n3 * gain[3:4, :] + shift[3:4, :]).astype(BF)
        stored = pool.start(out, out_o)
        e = cot[...].astype(F32)
        small[0] = jnp.zeros((SMALL_ROWS, d), F32)
        small[0, 9:10, :] = row_sum(e * n3)
        small[0, 13:14, :] = row_sum(e)
        eg = e * gain[3:4, :]
        dh[...] = r3 * (
            eg - jnp.mean(eg, axis=-1, keepdims=True) - n3 * jnp.mean(eg * n3, axis=-1, keepdims=True)
        )
        df[...] = dh[...].astype(BF)
        for i in range(4):
            gather(halving, r, i, 4, gat, perm)
            grad(halving, perm, df)
        small[0, 18:19, :] = row_sum(df[...])
        for j in range(max(0, steps - 2), steps):
            stores[j].wait()
        stored.wait()

    pl.run_scoped(
        feed_phase,
        pltpu.VMEM((2, t, d), BF),
        pltpu.VMEM((2, t, d), BF),
        pltpu.VMEM((steps * d, t), at.dtype),
        pltpu.VMEM(act, BF),
        pltpu.VMEM(act, BF),
    )

    def feed_back_phase(u, du, acc, h2):
        flight = [pool.start(u_h.at[j], u.at[j]) for j in range(2)]
        turned = pool.start(a2_h, raw)
        later = pool.start(h2_h, h2)
        for j in range(steps + 1):
            if j < steps:
                flight[j].wait()
                x = u[j % 2].astype(F32)
                x2 = x * x
                th = jnp.tanh(x * (GELU_C + GELU_D * x2))
                slope = (0.5 + 0.5 * th) * (1.0 + (1.0 - th) * (x * (GELU_C + (3 * GELU_D) * x2)))
                w = stream.take()
                y = dot_t(df[...], w[...]) * slope
                du[j] = y.astype(BF)
                small[0, 14 + j : 15 + j, :] = row_sum(y)
                if j + 2 < steps:
                    flight.append(pool.start(u_h.at[j + 2], u.at[j % 2]))
                spend(2.4)
            if j > 0:
                w = stream.take()
                z = dot_t(du[j - 1], w[...])
                if j == 1:
                    acc[...] = z
                else:
                    acc[...] += z
                spend(1.6)
                if j == 1:
                    turned.wait()
                    turn(halving, r, raw, at, perm)
                grad(halving, perm, du.at[j - 1])
        turned = pool.start(cc_h, raw)
        later.wait()
        back_, small[0, 8:9, :], small[0, 12:13, :] = norm_back(acc[...], h2[...], gain[2:3, :])
        dh[...] += back_
        dx[...] = dh[...].astype(BF)
        small[0, 5:6, :] = row_sum(dx[...])
        spend(1.2)
        w = stream.take()
        dc[...] = dot_t(dx[...], w[...]).astype(BF)
        spend(1.3)
        turned.wait()
        turn(halving, r, raw, at, perm)
        grad(halving, perm, dx)

    pl.run_scoped(
        feed_back_phase,
        pltpu.VMEM((2, t, d), BF),
        pltpu.VMEM((steps, t, d), BF),
        pltpu.VMEM(act, F32),
        pltpu.VMEM(act, F32),
    )

    def cross_back_phase(e, r_, q, k, v, c, dq, dk, dv, gm):
        loads = Group(pool)
        start_parts(loads, nb, ce, e, (cr, r_), (cc_h, c), (cv_h, v), (ck_h, k), (cq_h, q))
        turned = pool.start(a1_h, raw)
        later = pool.start(h1_h, gm)
        for i in range(PARTS):
            loads.wait(6)
            attend_back(nb, rows, cols, i, e, r_, q, k, v, c, dc, dq, dk, dv)
            spend(2.2)
        turned.wait()
        turn(halving, r, raw, at, perm)
        turned = Group(pool)
        for b in range(nb):
            turned.start(
                (memory.at[b, 0, frame], raw.at[pl.ds(b * cols, half)]),
                (far_mem.at[b], raw.at[pl.ds(b * cols + half, half)]),
            )
        grad(halving, perm, dq)
        w = stream.take()
        up_ = dot_t(dq[...], w[...])
        later.wait()
        back_, small[0, 7:8, :], small[0, 11:12, :] = norm_back(up_, gm[...], gain[1:2, :])
        dh[...] += back_
        dx[...] = dh[...].astype(BF)
        small[0, 2:3, :] = row_sum(dx[...])
        small[0, 3:4, :] = row_sum(dq[...])
        small[0, 4:5, :] = row_sum(dv[...])
        spend(2.6)
        turned.wait_all()
        turn(halving, r, raw, at, perm)
        turned = pool.start(sc, raw)
        grad(halving, perm, dk)
        grad(halving, perm, dv)
        w = stream.take()
        gm[...] = dot_t(dk[...], w[...])
        w = stream.take()
        gm[...] += dot_t(dv[...], w[...])
        spend(2.6)
        moves = []
        for b in range(nb):
            moves.append(pool.start(gm.at[pl.ds(b * cols, half)], gm_o.at[b, 0, frame]))
            far = halving.remote(
                gm.at[pl.ds(b * cols + half, half)], gm_o.at[b, 0, frame],
                (xsem.at[0, nb + b], xsem.at[1, nb + b]), halving.partners["xz"][0],
            )
            far.start()
            moves.append(far)
        w = stream.take()
        dc[...] = dot_t(dx[...], w[...]).astype(BF)
        spend(1.3)
        turned.wait()
        turn(halving, r, raw, at, perm)
        grad(halving, perm, dx)
        for x in moves:
            x.wait()

    pl.run_scoped(
        cross_back_phase,
        pltpu.VMEM(ce.shape, BF),
        pltpu.VMEM(act, F32),
        pltpu.VMEM(act, BF),
        pltpu.VMEM(macts, BF),
        pltpu.VMEM(macts, BF),
        pltpu.VMEM(act, BF),
        pltpu.VMEM(act, BF),
        pltpu.VMEM(macts, BF),
        pltpu.VMEM(macts, BF),
        pltpu.VMEM(macts, F32),
    )

    def self_back_phase(e, r_, q, k, v, c, dq, dk, dv, tok):
        loads = Group(pool)
        start_parts(loads, nb, se, e, (sr, r_), (sc, c), (sv, v), (sk, k), (sq, q))
        turned = pool.start(a0_h, raw)
        later = pool.start(tok_h, tok)
        for i in range(PARTS):
            loads.wait(6)
            attend_back(nb, rows, rows, i, e, r_, q, k, v, c, dc, dq, dk, dv)
            spend(2.2)
        turned.wait()
        turn(halving, r, raw, at, perm)
        grad(halving, perm, dq)
        gather(halving, r, 0, 1, at, perm)
        grad(halving, perm, dk)
        grad(halving, perm, dv)
        w = stream.take()
        up_ = dot_t(dq[...], w[...])
        w = stream.take()
        up_ += dot_t(dk[...], w[...])
        w = stream.take()
        up_ += dot_t(dv[...], w[...])
        later.wait()
        back_, small[0, 6:7, :], small[0, 10:11, :] = norm_back(up_, tok[...].astype(F32), gain[0:1, :])
        dh[...] += back_
        moved = pool.start(dh, gt_o)
        small[0, 0:1, :] = row_sum(dq[...])
        small[0, 1:2, :] = row_sum(dv[...])
        halving.small_start()
        spend(5.2)
        moved.wait()

    pl.run_scoped(self_back_phase, pltpu.VMEM(se.shape, BF), pltpu.VMEM(act, F32), *[pltpu.VMEM(act, BF)] * 8)
    halving.finish()
    done = pltpu.make_async_copy(small.at[halving.stages + 1], small_o, osem)
    done.start()
    done.wait()


def layer(n_dp, nb, tok_len, frm_len, bias, gain, shift, rb, eb, tok, memory, cot, w_in, w_out, we, wr):
    t, d = tok.shape
    ff = we.shape[1]
    n = 2 * n_dp
    r = d // n
    rows, half = t // nb, memory.shape[3]
    m = 2 * half * nb
    kind = BF if r % 16 == 0 else F32
    act, macts = (t, d), (m, d)
    sem = pltpu.SemaphoreType.DMA
    held = [hbm((nb, half, d), BF), hbm(act, F32), hbm(act, F32), hbm(act, F32), hbm(act, F32)]
    held += [hbm((nb, HEADS, rows, rows), BF), hbm((nb, HEADS, rows, 2 * half), BF), hbm((ff // d, t, d), BF)]
    held += [hbm(act, BF)] * 7 + [hbm(macts, BF)] * 2 + [hbm(act, BF)] * 2
    assert len(held) == HELD + 1
    return pl.pallas_call(
        functools.partial(layer_kernel, n_dp, nb),
        out_shape=[
            hbm(act, BF), hbm((4 * r, d), F32), hbm((r, ff), F32), hbm((2, 3, r, d), F32), hbm((2, r, d), F32),
            hbm((SMALL_ROWS, d), F32), hbm(act, F32), hbm(memory.shape, F32),
        ]
        + held,
        in_specs=[SM] * 2 + [VM] * 5 + [ANY] * 7,
        out_specs=[ANY] * (8 + len(held)),
        scratch_shapes=halving_scratch(n_dp, d, UNITS)
        + [
            pltpu.VMEM((4, d, d), BF),
            pltpu.VMEM(act, BF),
            pltpu.VMEM(act, F32),
            *[pltpu.VMEM(act, BF)] * 3,
            pltpu.VMEM((d, t), kind),
            pltpu.VMEM((d, t), BF),
            sem((15 + 4 * (ff // d) + 8,)),
            sem((160,)),
            sem((2, 2 * nb)),
            sem,
        ],
        compiler_params=pltpu.CompilerParams(vmem_limit_bytes=63 * 2**20, collective_id=0, has_side_effects=True),
        name="layer",
    )(tok_len, frm_len, bias, gain, shift, rb, eb, tok, memory, cot, w_in, w_out, we, wr)[:8]


def finish_kernel(n, count, small_h, *refs):
    ins, outs, few = refs[:count], refs[count : 2 * count], refs[2 * count : 2 * count + 5]
    small, bias, gain, shift, eb, rb = refs[2 * count + 5 : 2 * count + 11]
    bufs = refs[2 * count + 11 : -2]
    loads, stores = Copies(refs[-2]), Copies(refs[-1])
    loads.start((small_h, small), *zip(ins, bufs))
    loads.wait()
    me = 2 * lax.axis_index("dp") + lax.axis_index("frame")
    d = small.shape[1]
    w, wide = bias.shape[2], eb.shape[1]

    def window(rows, first, width):
        return pltpu.roll(rows, d - first, 1)[:, :width]

    mine = window(small[...], me * w, w)
    for i in range(3):
        bias[i] = jnp.concatenate([mine[i : i + 1], mine[3 + i : 4 + i]], axis=0)
    gain[...], shift[...] = mine[6:10], mine[10:14]
    rb[...] = mine[18:19]
    place = me * wide
    row = small[14:15, :]
    for i in range(1, n * wide // d):
        row = jnp.where(place // d == i, small[14 + i : 15 + i, :], row)
    eb[...] = window(row, place % d, wide)
    stores.start(*zip((bias, gain, shift, eb, rb), few))
    for buf, out in zip(bufs, outs):
        loads.wait()
        stores.start((buf, out))
    stores.wait_all()


def finish(n, ff, small, *arrays):
    d = small.shape[1]
    w = d // n
    count = len(arrays)
    few = [hbm((3, 2, w), F32), hbm((4, w), F32), hbm((4, w), F32), hbm((1, ff // n), F32), hbm((1, w), F32)]
    return pl.pallas_call(
        functools.partial(finish_kernel, n, count),
        out_shape=[hbm(x.shape, x.dtype) for x in arrays] + few,
        in_specs=[ANY] * (count + 1),
        out_specs=[ANY] * (count + 5),
        scratch_shapes=[pltpu.VMEM(x.shape, x.dtype) for x in (small, *few, *arrays)]
        + [pltpu.SemaphoreType.DMA((count + 1,)), pltpu.SemaphoreType.DMA((count + 5,))],
        compiler_params=params(),
        name="finish",
    )(small, *arrays)


def local(
    n_dp,
    tokens,
    memory,
    token_lengths,
    frame_lengths,
    attention_in,
    attention_out,
    attention_bias,
    norm_gain,
    norm_bias,
    expand_weight,
    expand_bias,
    reduce_weight,
    reduce_bias,
    cotangent,
):
    n = 2 * n_dp
    nb = tokens.shape[0]
    t = nb * tokens.shape[3]
    ff = expand_weight.shape[1]
    out, grad_reduce, grad_expand, grad_in, grad_out, small, grad_tokens, grad_memory = layer(
        n_dp, nb, token_lengths, frame_lengths, jnp.transpose(attention_bias, (1, 0, 2)), norm_gain, norm_bias,
        reduce_bias.reshape(1, D), expand_bias.reshape(1, ff), tokens.reshape(t, D), memory,
        cotangent.reshape(t, D), attention_in, attention_out, expand_weight, reduce_weight,
    )
    out, grad_tokens, grad_memory, grad_reduce, grad_expand, grad_in, grad_out, *rest = finish(
        n, ff, small, out, grad_tokens, grad_memory, grad_reduce, grad_expand, grad_in, grad_out
    )
    grad_bias, grad_gain, grad_shift, grad_eb, grad_rb = rest
    shape = tokens.shape
    return (
        out.reshape(shape),
        grad_tokens.reshape(shape),
        grad_memory,
        grad_in,
        grad_out,
        jnp.transpose(grad_bias, (1, 0, 2)),
        grad_gain,
        grad_shift,
        grad_expand,
        grad_eb.reshape(-1),
        grad_reduce,
        grad_rb.reshape(-1),
    )


def solution(mesh):
    spread = P(None, "dp", "frame", None, None)
    by_frame = P(None, "dp", None, "frame", None)
    both = ("dp", "frame")
    lengths = P(None, "dp", None, None)
    return jax.shard_map(
        functools.partial(local, mesh.shape["dp"]),
        mesh=mesh,
        in_specs=(spread, by_frame, lengths, lengths) + (P(),) * 9 + (spread,),
        out_specs=(
            spread,
            spread,
            by_frame,
            P(None, None, both, None),
            P(None, both, None),
            P(None, None, both),
            P(None, both),
            P(None, both),
            P(both, None),
            P(both),
            P(both, None),
            P(both),
        ),
        check_vma=False,
    )
```

```python
import functools
import math

import jax
import jax.numpy as jnp
from jax import lax
from jax.experimental import pallas as pl
from jax.experimental.pallas import tpu as pltpu
from jax.sharding import PartitionSpec as P

D = 1024
HEADS = 16
HEAD_DIM = 64
FACTOR = 1.0 / math.sqrt(HEAD_DIM)
BF = jnp.bfloat16
F32 = jnp.float32


def dot(a, b):
    return jnp.dot(a, b, preferred_element_type=F32)


def dot_t(a, b):
    return lax.dot_general(a, b, (((1,), (1,)), ((), ())), preferred_element_type=F32)


VM = pl.BlockSpec(memory_space=pltpu.VMEM)
SM = pl.BlockSpec(memory_space=pltpu.SMEM)
ANY = pl.BlockSpec(memory_space=pl.ANY)
GELU_C = 0.7978845608028654
GELU_D = 0.044715 * GELU_C


def params(mib=58):
    return pltpu.CompilerParams(vmem_limit_bytes=mib * 2**20)


def hbm(shape, kind):
    return jax.ShapeDtypeStruct(shape, kind)


class Copies:
    def __init__(self, sems):
        self.sems, self.copies, self.done = sems, [], 0

    def start(self, *pairs):
        for src, dst in pairs:
            copy = pltpu.make_async_copy(src, dst, self.sems.at[len(self.copies)])
            copy.start()
            self.copies.append(copy)

    def wait(self, count=1):
        for copy in self.copies[self.done : self.done + count]:
            copy.wait()
        self.done += count

    def wait_all(self):
        self.wait(len(self.copies) - self.done)


def stats(v):
    off = v - jnp.mean(v, axis=-1, keepdims=True)
    r = lax.rsqrt(jnp.mean(off * off, axis=-1, keepdims=True) + 1e-5)
    return off * r, r


def norm_back(e, v, gain):
    n, r = stats(v)
    eg = e * gain
    back = r * (
        eg - jnp.mean(eg, axis=-1, keepdims=True) - n * jnp.mean(eg * n, axis=-1, keepdims=True)
    )
    return back, row_sum(e * n), row_sum(e)


def row_sum(x):
    return jnp.sum(x.astype(F32), axis=0, keepdims=True)


def pair_mask(rows):
    return lax.broadcasted_iota(jnp.int32, (rows, 128), 1) < HEAD_DIM


def segments(lengths, b, a, shape, dim, shift=0):
    pos = lax.broadcasted_iota(jnp.int32, shape, dim) + shift
    pos = jnp.where(pos >= shape[dim], pos - shape[dim], pos)
    total, seg = 0, jnp.zeros(shape, jnp.int32)
    for i in range(lengths.shape[3] - 1):
        total = total + lengths[b, 0, a, i]
        seg = seg + (pos >= total).astype(jnp.int32)
    return seg


def attend(nb, rows, cols, part, q, k, v, e_ref, r_ref, c, mask):
    low = pair_mask(rows)
    one = jnp.ones((cols, 128), BF)

    for j in range(part * HEADS // 4, (part + 1) * HEADS // 4):
        lanes = pl.ds(j * 128, 128)
        for b in range(nb):
            qs, ks = pl.ds(b * rows, rows), pl.ds(b * cols, cols)
            q2, k2, v2 = q[qs, lanes], k[ks, lanes], v[ks, lanes]
            zero = jnp.zeros_like(q2)
            both = jnp.concatenate([jnp.where(low, q2, zero), jnp.where(low, zero, q2)], axis=0)
            s = dot_t(both, k2).reshape(2, rows, cols) + mask[b][None]
            e = jnp.exp(s - jnp.max(s, axis=-1, keepdims=True)).astype(BF)
            e_ref[b, pl.ds(2 * j, 2)] = e
            o = dot(e.reshape(2 * rows, cols), jnp.concatenate([v2, one], axis=1))
            r = 1.0 / jnp.where(low, o[:rows, 128:], o[rows:, 128:])
            r_ref[qs, lanes] = r.astype(BF)
            c[qs, lanes] = (jnp.where(low, o[:rows, :128], o[rows:, :128]) * r).astype(BF)


def attend_back(nb, rows, cols, part, e_ref, r_ref, q, k, v, c, dc, dq, dk, dv):
    low, low_k = pair_mask(rows), pair_mask(cols)
    minus = jnp.full((cols, 128), -1, BF)

    count = HEADS // 2 // PARTS
    for j in range(part * count, (part + 1) * count):
        lanes = pl.ds(j * 128, 128)
        for b in range(nb):
            qs, ks = pl.ds(b * rows, rows), pl.ds(b * cols, cols)
            q2, k2, v2 = q[qs, lanes], k[ks, lanes], v[ks, lanes]
            dcs = dc[qs, lanes].astype(F32) * r_ref[qs, lanes].astype(F32)
            delta = (dcs * c[qs, lanes].astype(F32)).astype(BF)
            dcs = dcs.astype(BF)
            zero = jnp.zeros_like(dcs)
            first = jnp.concatenate([jnp.where(low, dcs, zero), jnp.where(low, delta, zero)], axis=1)
            second = jnp.concatenate([jnp.where(low, zero, dcs), jnp.where(low, zero, delta)], axis=1)
            slope = dot_t(
                jnp.concatenate([first, second], axis=0), jnp.concatenate([v2, minus], axis=1)
            )
            e = e_ref[b, pl.ds(2 * j, 2)]
            ds = (e.astype(F32) * slope.reshape(2, rows, cols)).astype(BF)
            g = dot(ds.reshape(2 * rows, cols), k2)
            dq[qs, lanes] = (jnp.where(low, g[:rows], g[rows:]) * FACTOR).astype(BF)
            g = dot(jnp.concatenate([ds[0].T, ds[1].T], axis=0), q2)
            dk[ks, lanes] = jnp.where(low_k, g[:cols], g[cols:]).astype(BF)
            g = dot(jnp.concatenate([e[0].T, e[1].T], axis=0), dcs)
            dv[ks, lanes] = jnp.where(low_k, g[:cols], g[cols:]).astype(BF)


PARTS = 4


def start_parts(loads, nb, e_h, e, *pairs):
    for i in range(PARTS):
        heads = pl.ds(i * HEADS // PARTS, HEADS // PARTS)
        loads.start((e_h.at[:, heads], e.at[:, heads]))
        for src, dst in pairs:
            lanes = pl.ds(i * (D // PARTS), D // PARTS)
            loads.start((src.at[:, lanes], dst.at[:, lanes]))


K_SLOTS = 9
R_SLOTS = 6
S_SLOTS = 4
C_SLOTS = 4
F_SLOTS = 4
PERIOD = 6.3
START = 2.0


ORDERS = {
    "xz": ([0, 2, 1, 3], [1, 2, 0, 3]),
    "zx": ([2, 0, 1, 3], [2, 1, 0, 3]),
    "xy": ([0, 1, 2, 3], [1, 0, 2, 3]),
}


def stage_masks(n_dp, order):
    m = n_dp.bit_length() - 1
    if m == 4:
        orders = ORDERS[order]
    else:
        one = list(range(0, m, 2)) + list(range(1, m, 2))
        orders = one, one[1:] + one[:1]
    return [(1 << a, 1 << b) for a, b in zip(*orders)]


def place_masks(n_dp, order):
    masks = stage_masks(n_dp, order)
    m = len(masks)
    out = []
    for f in range(2):
        row = []
        for p in range(2 * n_dp):
            far = p >> m
            mask = far
            for s in range(m):
                if (p >> (m - 1 - s)) & 1:
                    mask ^= 2 * masks[s][1 - f if far else f]
            row.append(mask)
        out.append(row)
    return out


def shard_at(n_dp, order, dp, frame, p):
    masks = place_masks(n_dp, order)
    mine = total = 2 * dp + frame
    step = 1
    while step < 2 * n_dp:
        zero, one = (masks[0][p] // step) % 2, (masks[1][p] // step) % 2
        if zero or one:
            flips = step if zero == one else step * (zero + frame * (one - zero))
            total = total + flips * (1 - 2 * ((mine // step) % 2))
        step *= 2
    return total


class Halving:
    def __init__(self, n_dp, refs, outs, orders):
        self.n_dp, self.outs = n_dp, outs
        self.widths = [out.shape[1] for out in outs]
        self.units = len(outs)
        self.s, self.r0, self.k, self.r, self.kf, self.rf, self.fin = refs[:7]
        self.small, self.small_r, self.sems, self.small_sems, self.fin_sem = refs[7:]
        self.orders = orders
        self.stages = n_dp.bit_length() - 1
        self.lags = [0, 2, 4] + [stage + 2 for stage in range(3, self.stages + 1)]
        self.dp, self.frame = lax.axis_index("dp"), lax.axis_index("frame")
        self.partners = {
            order: [(self.dp, 1 - self.frame)] + [(self.flip(m), self.frame) for m in stage_masks(n_dp, order)]
            for order in ORDERS
        }
        self.started, self.waited, self.stored = [], set(), set()
        self.now, self.slot, self.made, self.core, self.ended = 0.0, 0, 0, 0, 0
        self.small_step = None

    def flip(self, mask):
        bit = mask[0] + self.frame * (mask[1] - mask[0])
        return self.dp + bit * (1 - 2 * ((self.dp // bit) % 2))

    def greet(self):
        barrier = pltpu.get_barrier_semaphore()
        for stage in range(self.stages + 1):
            pl.semaphore_signal(
                barrier, inc=1, device_id=self.partners["xz"][stage], device_id_type=pl.DeviceIdType.MESH
            )

    def meet(self):
        pl.semaphore_wait(pltpu.get_barrier_semaphore(), self.stages + 1)

    def rows(self, stage):
        return self.s.shape[1] >> stage

    def wide(self, stage):
        return stage > 0 and self.rows(stage) < 16

    def remote(self, src, dst, sems, partner):
        return pltpu.make_async_remote_copy(
            src_ref=src, dst_ref=dst, send_sem=sems[0], recv_sem=sems[1],
            device_id=partner, device_id_type=pl.DeviceIdType.MESH,
        )

    def copy(self, c, stage):
        h = self.rows(stage)
        half = pl.ds(h, h)
        if c is None:
            src, dst = self.small.at[stage], self.small_r.at[stage]
            sems = self.small_sems.at[0, stage], self.small_sems.at[1, stage]
        else:
            sems = self.sems.at[0, c, stage], self.sems.at[1, c, stage]
            lanes = pl.ds(0, self.widths[c])
            if stage == 0:
                src, dst = self.s.at[c % S_SLOTS, :, lanes], self.r0.at[c % C_SLOTS, :, lanes]
            elif self.wide(stage):
                src, dst = self.kf.at[c % K_SLOTS, half, lanes], self.rf.at[c % R_SLOTS, half, lanes]
            else:
                src, dst = self.k.at[c % K_SLOTS, half, lanes], self.r.at[c % R_SLOTS, half, lanes]
        return self.remote(src, dst, sems, self.partners["xz" if c is None else self.orders[c]][stage])

    def send(self, c, stage):
        self.started.append((c, stage))
        self.copy(c, stage).start()

    def sent(self, c, stage):
        if (c, stage) not in self.waited:
            self.waited.add((c, stage))
            self.copy(c, stage).wait_send()

    def store(self, c):
        return pltpu.make_async_copy(
            self.fin.at[c % F_SLOTS, :, pl.ds(0, self.widths[c])], self.outs[c], self.fin_sem.at[c]
        )

    def free(self, c):
        while self.core < c - 1:
            self.join()
        if c >= S_SLOTS:
            self.sent(c - S_SLOTS, 0)
        if c >= K_SLOTS:
            while self.ended <= c - K_SLOTS:
                self.step()
            for stage in range(1, self.stages + 1):
                self.sent(c - K_SLOTS, stage)

    def join(self):
        c = self.core
        assert c < self.made
        self.copy(c, 0).wait_recv()
        slot, lanes = c % K_SLOTS, pl.ds(0, self.widths[c])
        own, got = self.k[slot, :, lanes], self.r0[c % C_SLOTS, :, lanes]
        self.k[slot, :, lanes] = (own.astype(F32) + got.astype(F32)).astype(BF)
        self.core += 1
        self.now += 0.4

    def fold(self, c, stage):
        h = self.rows(stage)
        near, half = pl.ds(0, h), pl.ds(h, h)
        slot, slot_r, lanes = c % K_SLOTS, c % R_SLOTS, pl.ds(0, self.widths[c])
        self.copy(c, stage).wait_recv()
        if self.wide(stage):
            total = self.kf[slot, near, lanes] + self.rf[slot_r, half, lanes]
        else:
            total = self.k[slot, near, lanes].astype(F32) + self.r[slot_r, half, lanes].astype(F32)
        if stage == self.stages:
            if c >= F_SLOTS:
                self.stored.add(c - F_SLOTS)
                self.store(c - F_SLOTS).wait()
            self.fin[c % F_SLOTS, :, lanes] = total
            self.store(c).start()
            self.ended = c + 1
            return
        if self.wide(stage + 1):
            self.kf[slot, near, lanes] = total
        else:
            self.k[slot, near, lanes] = total.astype(BF)
        self.send(c, stage + 1)

    def small_start(self):
        self.small_step = 0
        self.send(None, 0)

    def step(self):
        k = self.slot
        self.slot += 1
        if k < self.units:
            while self.core <= k:
                self.join()
            self.send(k, 1)
        for stage in range(1, self.stages + 1):
            c = k - self.lags[stage]
            if 0 <= c < self.units:
                self.fold(c, stage)
                self.now += 0.25
        self.small_fold()

    def small_fold(self):
        stage = self.small_step
        if stage is None or stage > self.stages:
            return
        self.copy(None, stage).wait_recv()
        self.small[stage + 1] = self.small[stage] + self.small_r[stage]
        self.small_step += 1
        if stage < self.stages:
            self.send(None, stage + 1)

    def spend(self, us):
        self.now += us
        while self.slot < self.made and START + PERIOD * sum(self.widths[: self.slot]) / D <= self.now:
            self.step()

    def finish(self):
        while self.ended < self.units:
            self.step()
        while self.small_step <= self.stages:
            self.small_fold()
        for c, stage in self.started:
            self.sent(c, stage)
        for c in range(self.units):
            if c not in self.stored:
                self.store(c).wait()


def halving_scratch(n_dp, d, units):
    n = 2 * n_dp
    m = d // 2
    stages = n_dp.bit_length() - 1
    sem = pltpu.SemaphoreType.DMA
    wide = (m >> stages) < 16
    return [
        pltpu.VMEM((S_SLOTS, m, d), BF),
        pltpu.VMEM((C_SLOTS, m, d), BF),
        pltpu.VMEM((K_SLOTS, m, d), BF),
        pltpu.VMEM((R_SLOTS, m, d), BF),
        pltpu.VMEM((K_SLOTS, 16, d) if wide else (1, 8, 128), F32),
        pltpu.VMEM((R_SLOTS, 16, d) if wide else (1, 8, 128), F32),
        pltpu.VMEM((F_SLOTS, d // n, d), F32),
        pltpu.VMEM((stages + 2, 24, d), F32),
        pltpu.VMEM((stages + 1, 24, d), F32),
        sem((2, units, stages + 1)),
        sem((2, stages + 1)),
        sem((units,)),
    ]


class Pool:
    def __init__(self, sems):
        self.sems, self.used = sems, 0

    def start(self, src, dst):
        copy = pltpu.make_async_copy(src, dst, self.sems.at[self.used])
        self.used += 1
        copy.start()
        return copy


class Group:
    def __init__(self, pool):
        self.pool, self.copies, self.done = pool, [], 0

    def start(self, *pairs):
        for src, dst in pairs:
            self.copies.append(self.pool.start(src, dst))

    def wait(self, count):
        for copy in self.copies[self.done : self.done + count]:
            copy.wait()
        self.done += count

    def wait_all(self):
        self.wait(len(self.copies) - self.done)


class Stream:
    def __init__(self, blocks, buf, sems):
        self.blocks, self.buf, self.sems = blocks, buf, sems
        self.depth, self.taken = buf.shape[0], 0
        for i in range(self.depth - 1):
            self.copy(i).start()

    def copy(self, i):
        return pltpu.make_async_copy(self.blocks[i](), self.buf.at[i % self.depth], self.sems.at[i])

    def take(self):
        i = self.taken
        self.taken += 1
        ahead = i + self.depth - 2
        if i > 0 and ahead < len(self.blocks):
            if ahead >= self.depth - 1:
                self.copy(ahead).start()
        self.copy(i).wait()
        return self.buf.at[i % self.depth]


def store_half(stores, part, heads, *pairs):
    some = pl.ds(part * HEADS // 2, HEADS // 2)
    stores.start((heads[0].at[:, some], heads[1].at[:, some]))
    lanes = pl.ds(part * D // 2, D // 2)
    for src, dst in pairs:
        stores.start((src.at[:, lanes], dst.at[:, lanes]))


def turn(halving, r, src, at, perm):
    at[...] = src[...].T.astype(at.dtype)
    gather(halving, r, 0, 1, at, perm)


def gather(halving, r, u, count, at, perm):
    order = halving.orders[halving.made]
    for p in range(2 * halving.n_dp):
        base = shard_at(halving.n_dp, order, halving.dp, halving.frame, p) * (r * count)
        perm[pl.ds(p * r, r), :] = at[pl.ds(pl.multiple_of(base + u * r, 8), r), :].astype(perm.dtype)
    halving.spend(0.5)


def grad(halving, left, right):
    c = halving.made
    m = left.shape[0] // 2
    wide = right.shape[1]
    lanes = pl.ds(0, wide)
    assert wide == halving.widths[c]
    halving.free(c)
    halving.s[c % S_SLOTS, :, lanes] = dot(left[pl.ds(m, m), :], right[...]).astype(BF)
    halving.send(c, 0)
    halving.k[c % K_SLOTS, :, lanes] = dot(left[pl.ds(0, m), :], right[...]).astype(BF)
    halving.made += 1
    halving.spend(1.4 * wide / D)


SMALL_ROWS = 24
UNITS = 16
HELD = 18


def layer_kernel(n_dp, nb, *refs):
    (
        tok_len, frm_len, bias, gain, shift, rb, eb,
        tok_h, memory, cot_h, w_in, w_out, we, wr,
    ) = refs[:14]
    out_o, red_o, exp_o, in_o, out_w, small_o, gt_o, gm_o = refs[14:22]
    (
        far_mem, h1_h, h2_h, sr, cr, se, ce, u_h, sq, sk, sv, sc, a0_h, a1_h, cq_h, ck_h, cv_h, cc_h,
    ) = refs[22 : 22 + HELD]
    a2_h = refs[22 + HELD]
    rest = refs[23 + HELD :]
    hrefs = rest[:12]
    wbuf, df, dh, dx, dc, raw, at, perm, wsem, lsem, xsem, osem = rest[12:]
    t, d = df.shape
    steps = we.shape[1] // d
    r = d // (2 * n_dp)
    rows = t // nb
    half = memory.shape[3]
    cols = 2 * half
    act, macts = (t, d), (nb * cols, d)
    outs = [red_o.at[pl.ds(u * r, r)] for u in range(4)]
    outs += [exp_o.at[:, pl.ds(u * d, d)] for u in range(4)]
    outs += [out_w.at[1], in_o.at[1, 0], in_o.at[1, 1], in_o.at[1, 2]]
    outs += [out_w.at[0], in_o.at[0, 0], in_o.at[0, 1], in_o.at[0, 2]]
    halving = Halving(n_dp, hrefs, outs, ["xz"] * (UNITS - 2) + ["xy"] * 2)
    small = halving.small
    pool = Pool(lsem)
    spend = halving.spend
    frame = halving.frame

    up = [lambda j=j: we.at[:, pl.ds(j * d, d)] for j in range(steps)]
    down = [lambda j=j: wr.at[pl.ds(j * d, d)] for j in range(steps)]
    own = [[lambda i=i, j=j: w_in.at[i, j] for j in range(3)] for i in range(2)]
    back = [lambda i=i: w_out.at[i] for i in range(2)]
    blocks = [*own[0], back[0], *own[1], back[1]]
    for j in range(steps + 1):
        blocks += up[j : j + 1] + (down[j - 1 : j] if j else [])
    for j in range(steps + 1):
        blocks += down[j : j + 1] + (up[j - 1 : j] if j else [])
    blocks += [back[1], *own[1], back[0], *own[0]]

    def swap(b):
        return halving.remote(
            memory.at[b, 0, 1 - frame], far_mem.at[b], (xsem.at[0, b], xsem.at[1, b]), halving.partners["xz"][0]
        )

    def attention_phase(tok, mem, a0, q, k, v, c, e, r_, mask):
        first = pool.start(tok_h, tok)
        stream = Stream(blocks, wbuf, wsem)
        halving.greet()
        own_mem = [pool.start(memory.at[b, 0, frame], mem.at[pl.ds(b * cols, half)]) for b in range(nb)]
        square = (rows, rows)
        causal = lax.broadcasted_iota(jnp.int32, square, 1) <= lax.broadcasted_iota(jnp.int32, square, 0)
        for b in range(nb):
            same = segments(tok_len, b, frame, square, 0) == segments(tok_len, b, frame, square, 1)
            mask[b] = jnp.where(same & causal, 0.0, -1e30)
        first.wait()
        n0, _ = stats(tok[...].astype(F32))
        a0[...] = (n0 * gain[0:1, :] + shift[0:1, :]).astype(BF)
        w = stream.take()
        q[...] = ((dot(a0[...], w[...]) + bias[0, 0:1, :]).astype(BF).astype(F32) * FACTOR).astype(BF)
        w = stream.take()
        k[...] = dot(a0[...], w[...]).astype(BF)
        w = stream.take()
        v[...] = (dot(a0[...], w[...]) + bias[1, 0:1, :]).astype(BF)
        stores = Group(pool)
        stores.start((a0, a0_h), (q, sq), (k, sk), (v, sv))
        halving.meet()
        for b in range(nb):
            swap(b).start()
        for i in range(2):
            attend(nb, rows, rows, i, q, k, v, e, r_, c, mask)
            store_half(stores, i, (e, se), (r_, sr), (c, sc))
        w = stream.take()
        dh[...] = tok[...].astype(F32) + dot(c[...], w[...]) + bias[2, 0:1, :]
        n1, _ = stats(dh[...])
        raw[...] = (n1 * gain[1:2, :] + shift[1:2, :]).astype(BF)
        kept = Group(pool)
        kept.start((dh, h1_h), (raw, a1_h))
        for b in range(nb):
            swap(b).wait_recv()
        theirs = [pool.start(far_mem.at[b], mem.at[pl.ds(b * cols + half, half)]) for b in range(nb)]
        w = stream.take()
        dx[...] = ((dot(raw[...], w[...]) + bias[0, 1:2, :]).astype(BF).astype(F32) * FACTOR).astype(BF)
        kept.start((dx, cq_h))
        for x in own_mem:
            x.wait()
        shape = (rows, cols)
        for b in range(nb):
            same = segments(tok_len, b, frame, shape, 0) == segments(frm_len, b, frame, shape, 1, frame * half)
            mask[b] = jnp.where(same, 0.0, -1e30)
        stores.wait(4)
        for x in theirs:
            x.wait()
        w = stream.take()
        k[...] = dot(mem[...], w[...]).astype(BF)
        w = stream.take()
        v[...] = (dot(mem[...], w[...]) + bias[1, 1:2, :]).astype(BF)
        stores.wait_all()
        stores.start((k, ck_h), (v, cv_h))
        for i in range(2):
            attend(nb, rows, cols, i, dx, k, v, e, r_, c, mask)
            store_half(stores, i, (e, ce), (r_, cr), (c, cc_h))
        kept.wait_all()
        w = stream.take()
        dh[...] += dot(c[...], w[...]) + bias[2, 1:2, :]
        n2, _ = stats(dh[...])
        raw[...] = (n2 * gain[2:3, :] + shift[2:3, :]).astype(BF)
        for b in range(nb):
            swap(b).wait_send()
        stores.wait_all()
        return stream.taken

    stream_at = []

    def run_attention(*scratch):
        stream_at.append(attention_phase(*scratch))

    pl.run_scoped(
        run_attention,
        *[pltpu.VMEM(act, BF), pltpu.VMEM(macts, BF)],
        *[pltpu.VMEM(act, BF)] * 5,
        pltpu.VMEM(se.shape, BF),
        pltpu.VMEM(act, BF),
        pltpu.VMEM((nb, rows, cols), F32),
    )

    class Rest(Stream):
        def __init__(self):
            self.blocks, self.buf, self.sems = blocks, wbuf, wsem
            self.depth, self.taken = wbuf.shape[0], stream_at[0]

    stream = Rest()

    def feed_phase(u, g, gat, cot, out):
        later = pool.start(cot_h, cot)
        kept = [pool.start(dh, h2_h), pool.start(raw, a2_h)]
        stores = {}
        for j in range(steps + 1):
            if j < steps:
                w = stream.take()
                x = dot(raw[...], w[...]) + eb[:, j * d : (j + 1) * d]
                if j >= 2:
                    stores[j - 2].wait()
                u[j % 2] = x.astype(BF)
                g[j % 2] = (0.5 * x * (1.0 + jnp.tanh(x * (GELU_C + GELU_D * (x * x))))).astype(BF)
                stores[j] = pool.start(u.at[j % 2], u_h.at[j])
            if j > 0:
                w = stream.take()
                y = dot(g[(j - 1) % 2], w[...])
                if j == 1:
                    for x in kept:
                        x.wait()
                    dh[...] += y + rb[...]
                else:
                    dh[...] += y
                gat[pl.ds((j - 1) * d, d), :] = g[(j - 1) % 2].T.astype(gat.dtype)
        later.wait()
        n3, r3 = stats(dh[...])
        out[...] = (n3 * gain[3:4, :] + shift[3:4, :]).astype(BF)
        stored = pool.start(out, out_o)
        e = cot[...].astype(F32)
        small[0] = jnp.zeros((SMALL_ROWS, d), F32)
        small[0, 9:10, :] = row_sum(e * n3)
        small[0, 13:14, :] = row_sum(e)
        eg = e * gain[3:4, :]
        dh[...] = r3 * (
            eg - jnp.mean(eg, axis=-1, keepdims=True) - n3 * jnp.mean(eg * n3, axis=-1, keepdims=True)
        )
        df[...] = dh[...].astype(BF)
        for i in range(4):
            gather(halving, r, i, 4, gat, perm)
            grad(halving, perm, df)
        small[0, 18:19, :] = row_sum(df[...])
        for j in range(max(0, steps - 2), steps):
            stores[j].wait()
        stored.wait()

    pl.run_scoped(
        feed_phase,
        pltpu.VMEM((2, t, d), BF),
        pltpu.VMEM((2, t, d), BF),
        pltpu.VMEM((steps * d, t), at.dtype),
        pltpu.VMEM(act, BF),
        pltpu.VMEM(act, BF),
    )

    def feed_back_phase(u, du, acc, h2):
        flight = [pool.start(u_h.at[j], u.at[j]) for j in range(2)]
        turned = pool.start(a2_h, raw)
        later = pool.start(h2_h, h2)
        for j in range(steps + 1):
            if j < steps:
                flight[j].wait()
                x = u[j % 2].astype(F32)
                x2 = x * x
                th = jnp.tanh(x * (GELU_C + GELU_D * x2))
                slope = (0.5 + 0.5 * th) * (1.0 + (1.0 - th) * (x * (GELU_C + (3 * GELU_D) * x2)))
                w = stream.take()
                y = dot_t(df[...], w[...]) * slope
                du[j] = y.astype(BF)
                small[0, 14 + j : 15 + j, :] = row_sum(y)
                if j + 2 < steps:
                    flight.append(pool.start(u_h.at[j + 2], u.at[j % 2]))
                spend(2.4)
            if j > 0:
                w = stream.take()
                z = dot_t(du[j - 1], w[...])
                if j == 1:
                    acc[...] = z
                else:
                    acc[...] += z
                spend(1.6)
                if j == 1:
                    turned.wait()
                    turn(halving, r, raw, at, perm)
                grad(halving, perm, du.at[j - 1])
        turned = pool.start(cc_h, raw)
        later.wait()
        back_, small[0, 8:9, :], small[0, 12:13, :] = norm_back(acc[...], h2[...], gain[2:3, :])
        dh[...] += back_
        dx[...] = dh[...].astype(BF)
        small[0, 5:6, :] = row_sum(dx[...])
        spend(1.2)
        w = stream.take()
        dc[...] = dot_t(dx[...], w[...]).astype(BF)
        spend(1.3)
        turned.wait()
        turn(halving, r, raw, at, perm)
        grad(halving, perm, dx)

    pl.run_scoped(
        feed_back_phase,
        pltpu.VMEM((2, t, d), BF),
        pltpu.VMEM((steps, t, d), BF),
        pltpu.VMEM(act, F32),
        pltpu.VMEM(act, F32),
    )

    def cross_back_phase(e, r_, q, k, v, c, dq, dk, dv, gm):
        loads = Group(pool)
        start_parts(loads, nb, ce, e, (cr, r_), (cc_h, c), (cv_h, v), (ck_h, k), (cq_h, q))
        turned = pool.start(a1_h, raw)
        later = pool.start(h1_h, gm)
        for i in range(PARTS):
            loads.wait(6)
            attend_back(nb, rows, cols, i, e, r_, q, k, v, c, dc, dq, dk, dv)
            spend(2.2)
        turned.wait()
        turn(halving, r, raw, at, perm)
        turned = Group(pool)
        for b in range(nb):
            turned.start(
                (memory.at[b, 0, frame], raw.at[pl.ds(b * cols, half)]),
                (far_mem.at[b], raw.at[pl.ds(b * cols + half, half)]),
            )
        grad(halving, perm, dq)
        w = stream.take()
        up_ = dot_t(dq[...], w[...])
        later.wait()
        back_, small[0, 7:8, :], small[0, 11:12, :] = norm_back(up_, gm[...], gain[1:2, :])
        dh[...] += back_
        dx[...] = dh[...].astype(BF)
        small[0, 2:3, :] = row_sum(dx[...])
        small[0, 3:4, :] = row_sum(dq[...])
        small[0, 4:5, :] = row_sum(dv[...])
        spend(2.6)
        turned.wait_all()
        turn(halving, r, raw, at, perm)
        turned = pool.start(sc, raw)
        grad(halving, perm, dk)
        grad(halving, perm, dv)
        w = stream.take()
        gm[...] = dot_t(dk[...], w[...])
        w = stream.take()
        gm[...] += dot_t(dv[...], w[...])
        spend(2.6)
        moves = []
        for b in range(nb):
            moves.append(pool.start(gm.at[pl.ds(b * cols, half)], gm_o.at[b, 0, frame]))
            far = halving.remote(
                gm.at[pl.ds(b * cols + half, half)], gm_o.at[b, 0, frame],
                (xsem.at[0, nb + b], xsem.at[1, nb + b]), halving.partners["xz"][0],
            )
            far.start()
            moves.append(far)
        w = stream.take()
        dc[...] = dot_t(dx[...], w[...]).astype(BF)
        spend(1.3)
        turned.wait()
        turn(halving, r, raw, at, perm)
        grad(halving, perm, dx)
        for x in moves:
            x.wait()

    pl.run_scoped(
        cross_back_phase,
        pltpu.VMEM(ce.shape, BF),
        pltpu.VMEM(act, BF),
        pltpu.VMEM(act, BF),
        pltpu.VMEM(macts, BF),
        pltpu.VMEM(macts, BF),
        pltpu.VMEM(act, BF),
        pltpu.VMEM(act, BF),
        pltpu.VMEM(macts, BF),
        pltpu.VMEM(macts, BF),
        pltpu.VMEM(macts, F32),
    )

    def self_back_phase(e, r_, q, k, v, c, dq, dk, dv, tok):
        loads = Group(pool)
        start_parts(loads, nb, se, e, (sr, r_), (sc, c), (sv, v), (sk, k), (sq, q))
        turned = pool.start(a0_h, raw)
        later = pool.start(tok_h, tok)
        for i in range(PARTS):
            loads.wait(6)
            attend_back(nb, rows, rows, i, e, r_, q, k, v, c, dc, dq, dk, dv)
            spend(2.2)
        turned.wait()
        turn(halving, r, raw, at, perm)
        grad(halving, perm, dq)
        gather(halving, r, 0, 1, at, perm)
        grad(halving, perm, dk)
        grad(halving, perm, dv)
        w = stream.take()
        up_ = dot_t(dq[...], w[...])
        w = stream.take()
        up_ += dot_t(dk[...], w[...])
        w = stream.take()
        up_ += dot_t(dv[...], w[...])
        later.wait()
        back_, small[0, 6:7, :], small[0, 10:11, :] = norm_back(up_, tok[...].astype(F32), gain[0:1, :])
        dh[...] += back_
        moved = pool.start(dh, gt_o)
        small[0, 0:1, :] = row_sum(dq[...])
        small[0, 1:2, :] = row_sum(dv[...])
        halving.small_start()
        spend(5.2)
        moved.wait()

    pl.run_scoped(self_back_phase, pltpu.VMEM(se.shape, BF), *[pltpu.VMEM(act, BF)] * 9)
    halving.finish()
    done = pltpu.make_async_copy(small.at[halving.stages + 1], small_o, osem)
    done.start()
    done.wait()


def layer(n_dp, nb, tok_len, frm_len, bias, gain, shift, rb, eb, tok, memory, cot, w_in, w_out, we, wr):
    t, d = tok.shape
    ff = we.shape[1]
    n = 2 * n_dp
    r = d // n
    rows, half = t // nb, memory.shape[3]
    m = 2 * half * nb
    kind = BF if r % 16 == 0 else F32
    act, macts = (t, d), (m, d)
    sem = pltpu.SemaphoreType.DMA
    held = [hbm((nb, half, d), BF), hbm(act, F32), hbm(act, F32), hbm(act, BF), hbm(act, BF)]
    held += [hbm((nb, HEADS, rows, rows), BF), hbm((nb, HEADS, rows, 2 * half), BF), hbm((ff // d, t, d), BF)]
    held += [hbm(act, BF)] * 7 + [hbm(macts, BF)] * 2 + [hbm(act, BF)] * 2
    assert len(held) == HELD + 1
    return pl.pallas_call(
        functools.partial(layer_kernel, n_dp, nb),
        out_shape=[
            hbm(act, BF), hbm((4 * r, d), F32), hbm((r, ff), F32), hbm((2, 3, r, d), F32), hbm((2, r, d), F32),
            hbm((SMALL_ROWS, d), F32), hbm(act, F32), hbm(memory.shape, F32),
        ]
        + held,
        in_specs=[SM] * 2 + [VM] * 5 + [ANY] * 7,
        out_specs=[ANY] * (8 + len(held)),
        scratch_shapes=halving_scratch(n_dp, d, UNITS)
        + [
            pltpu.VMEM((4, d, d), BF),
            pltpu.VMEM(act, BF),
            pltpu.VMEM(act, F32),
            *[pltpu.VMEM(act, BF)] * 3,
            pltpu.VMEM((d, t), kind),
            pltpu.VMEM((d, t), BF),
            sem((15 + 4 * (ff // d) + 8,)),
            sem((160,)),
            sem((2, 2 * nb)),
            sem,
        ],
        compiler_params=pltpu.CompilerParams(vmem_limit_bytes=63 * 2**20, collective_id=0, has_side_effects=True),
        name="layer",
    )(tok_len, frm_len, bias, gain, shift, rb, eb, tok, memory, cot, w_in, w_out, we, wr)[:8]


def finish_kernel(n, count, small_h, *refs):
    ins, outs, few = refs[:count], refs[count : 2 * count], refs[2 * count : 2 * count + 5]
    small, bias, gain, shift, eb, rb = refs[2 * count + 5 : 2 * count + 11]
    bufs = refs[2 * count + 11 : -2]
    loads, stores = Copies(refs[-2]), Copies(refs[-1])
    loads.start((small_h, small), *zip(ins, bufs))
    loads.wait()
    me = 2 * lax.axis_index("dp") + lax.axis_index("frame")
    d = small.shape[1]
    w, wide = bias.shape[2], eb.shape[1]

    def window(rows, first, width):
        return pltpu.roll(rows, d - first, 1)[:, :width]

    mine = window(small[...], me * w, w)
    for i in range(3):
        bias[i] = jnp.concatenate([mine[i : i + 1], mine[3 + i : 4 + i]], axis=0)
    gain[...], shift[...] = mine[6:10], mine[10:14]
    rb[...] = mine[18:19]
    place = me * wide
    row = small[14:15, :]
    for i in range(1, n * wide // d):
        row = jnp.where(place // d == i, small[14 + i : 15 + i, :], row)
    eb[...] = window(row, place % d, wide)
    stores.start(*zip((bias, gain, shift, eb, rb), few))
    for buf, out in zip(bufs, outs):
        loads.wait()
        stores.start((buf, out))
    stores.wait_all()


def finish(n, ff, small, *arrays):
    d = small.shape[1]
    w = d // n
    count = len(arrays)
    few = [hbm((3, 2, w), F32), hbm((4, w), F32), hbm((4, w), F32), hbm((1, ff // n), F32), hbm((1, w), F32)]
    return pl.pallas_call(
        functools.partial(finish_kernel, n, count),
        out_shape=[hbm(x.shape, x.dtype) for x in arrays] + few,
        in_specs=[ANY] * (count + 1),
        out_specs=[ANY] * (count + 5),
        scratch_shapes=[pltpu.VMEM(x.shape, x.dtype) for x in (small, *few, *arrays)]
        + [pltpu.SemaphoreType.DMA((count + 1,)), pltpu.SemaphoreType.DMA((count + 5,))],
        compiler_params=params(),
        name="finish",
    )(small, *arrays)


def local(
    n_dp,
    tokens,
    memory,
    token_lengths,
    frame_lengths,
    attention_in,
    attention_out,
    attention_bias,
    norm_gain,
    norm_bias,
    expand_weight,
    expand_bias,
    reduce_weight,
    reduce_bias,
    cotangent,
):
    n = 2 * n_dp
    nb = tokens.shape[0]
    t = nb * tokens.shape[3]
    ff = expand_weight.shape[1]
    out, grad_reduce, grad_expand, grad_in, grad_out, small, grad_tokens, grad_memory = layer(
        n_dp, nb, token_lengths, frame_lengths, jnp.transpose(attention_bias, (1, 0, 2)), norm_gain, norm_bias,
        reduce_bias.reshape(1, D), expand_bias.reshape(1, ff), tokens.reshape(t, D), memory,
        cotangent.reshape(t, D), attention_in, attention_out, expand_weight, reduce_weight,
    )
    out, grad_tokens, grad_memory, grad_reduce, grad_expand, grad_in, grad_out, *rest = finish(
        n, ff, small, out, grad_tokens, grad_memory, grad_reduce, grad_expand, grad_in, grad_out
    )
    grad_bias, grad_gain, grad_shift, grad_eb, grad_rb = rest
    shape = tokens.shape
    return (
        out.reshape(shape),
        grad_tokens.reshape(shape),
        grad_memory,
        grad_in,
        grad_out,
        jnp.transpose(grad_bias, (1, 0, 2)),
        grad_gain,
        grad_shift,
        grad_expand,
        grad_eb.reshape(-1),
        grad_reduce,
        grad_rb.reshape(-1),
    )


def solution(mesh):
    spread = P(None, "dp", "frame", None, None)
    by_frame = P(None, "dp", None, "frame", None)
    both = ("dp", "frame")
    lengths = P(None, "dp", None, None)
    return jax.shard_map(
        functools.partial(local, mesh.shape["dp"]),
        mesh=mesh,
        in_specs=(spread, by_frame, lengths, lengths) + (P(),) * 9 + (spread,),
        out_specs=(
            spread,
            spread,
            by_frame,
            P(None, None, both, None),
            P(None, both, None),
            P(None, None, both),
            P(None, both),
            P(None, both),
            P(both, None),
            P(both),
            P(both, None),
            P(both),
        ),
        check_vma=False,
    )
```
